32 devices in a mesh: dp: 4 (over y, x), expert: 8 (over z, core).
Axes of the slice: x: 2, y: 2, z: 4, core: 2. Of those that a mesh axis runs over, the one named last changes fastest.
Arguments:
- tokens: bfloat16 [2048, 4096], P('expert', 'dp'), may hold values from -6 to 6
- gate_weight: bfloat16 [64, 4096, 768], P('expert', 'dp'), may hold values from -0.09375 to 0.09375
- up_weight: bfloat16 [64, 4096, 768], P('expert', 'dp'), may hold values from -0.09375 to 0.09375
- down_weight: bfloat16 [64, 768, 4096], P('expert', None, 'dp'), may hold values from -0.21875 to 0.21875
- routes: int32 [2048, 8], P('expert'), may hold values from 0 to 63, all different within a row; in each aligned block of 256 rows (0 to 255, 256 to 511, ...) at most 40 rows name the same one
- gate_levels: int32 [2048, 8], P('expert'), may hold values from 1 to 255
- log_ratio: float32 [2048], P('expert'), may hold values from -3 to 3
- cotangent: bfloat16 [2048, 4096], P('expert', 'dp'), may hold values from -6 to 6
Outputs:
- mixed_out: bfloat16 [2048, 4096], P('expert', 'dp')
- token_grad: bfloat16 [2048, 4096], P('expert', 'dp')
- gate_grad: float32 [2048, 8], P('expert')
The draws below stay inside these ranges and needn't reach their ends.
Inputs may be any that keep to these rules, and one draw needn't show every extreme that they name: `routes`: each row names 8 different experts; within the rows of one index of expert (aligned blocks of 256 rows) no expert is named more than 40 times, a bound that some block reaches.
All inputs are finite; a program needn't handle non-finite values.
Results may differ from the reference program's by a relative error of at most 0.014.
Values may be sent and summed in bfloat16 or wider, within the bound.
No kernel may reach another device: no remote copies, remote signals or barrier semaphores. Data moves between devices by JAX's collectives and lax.ppermute only.
A program may use at most 192 MiB of HBM per device.

```python
import math
import jax
import jax.numpy as jnp
import numpy as np
from jax import lax

D = 4096
FFW = 768
EXPERTS = 64
TOPK = 8
TOK_DEV = 256
CAP = 40
TOKENS = 2048
N_EXPERT = 8


def touch_ends(entries, stream_key, smallest, top_value):
    longest = entries.shape.index(max(entries.shape))
    spots = []
    for shift in (0, 1):
        where = [jax.random.randint(jax.random.fold_in(stream_key, axis), (), 0, length) for axis, length in enumerate(entries.shape)]
        where[longest] = (where[longest] + shift) % entries.shape[longest]
        spots.append(tuple(where))
    return entries.at[spots[0]].set(smallest).at[spots[1]].set(top_value)


def shard_levels(own_key, extent, cuts, low, top_value):
    factor_of = 1.0
    for axis_at, shards_of in cuts:
        steps = jax.random.uniform(jax.random.fold_in(jax.random.fold_in(own_key, 6), axis_at), (shards_of,), jnp.float32, low / len(cuts), top_value / len(cuts))
        factor_of = factor_of * jnp.repeat(jnp.exp(steps), extent[axis_at] // shards_of).reshape((-1,) + (1,) * (len(extent) - 1 - axis_at))
    return factor_of


def deal_out(key, own, number, rows, amount, top, reach, slope):
    sequence = jax.random.permutation(key, amount)
    packed, usual = shares(amount, rows * top, reach, slope, True), shares(amount, rows * top, reach, slope, False)
    places = jnp.arange(amount)

    def named(sizes, turn):
        used = int((sizes > 0).sum())
        fixed = max(1, used // 4)
        shifted = fixed + (places - fixed + turn * (used - fixed)) % max(1, amount - fixed)
        return jnp.zeros((amount,), jnp.int32).at[sequence[jnp.where(places < fixed, places, shifted)]].set(jnp.asarray(sizes, jnp.int32))

    sizes = jnp.where(number % 4 == 0, named(packed, number // 4), named(usual, number - number // 4 - 1))
    mixed = jax.random.permutation(jax.random.fold_in(own, 3), amount)
    donor, receiver = mixed[0:amount // 2 * 2:2], mixed[1:amount // 2 * 2:2]
    margin = jnp.minimum(sizes[donor] - 1, reach - sizes[receiver]) // 2
    margin = jnp.where((donor == sequence[0]) | (receiver == sequence[0]) | (sizes[receiver] == 0), 0, jnp.maximum(margin, 0))
    shifted = jax.random.randint(jax.random.fold_in(own, 4), (amount // 2,), 0, 1 << 20) % (margin + 1)
    sizes = sizes.at[donor].add(-shifted).at[receiver].add(shifted)
    members = jnp.searchsorted(jnp.cumsum(sizes), jnp.arange(rows * top), side="right").astype(jnp.int32)
    table = members.reshape(top, rows).T
    table = table[jax.random.permutation(jax.random.fold_in(own, 1), rows)]
    turn = jax.random.randint(jax.random.fold_in(own, 2), (rows, 1), 0, top)
    return jnp.take_along_axis(table, (jnp.arange(top)[None, :] + turn) % top, axis=1)


def shares(count, total, reach, skew, full):
    portions = [(1 << 20) // math.isqrt(standing ** skew) + 1 for standing in range(1, count + 1)]
    largest = reach if full else min(reach, max(-(-total // count), total * portions[0] // sum(portions)))
    least = 1 if total - largest >= count - 1 else 0
    holding, rest = [largest] + [least] * (count - 1), total - largest - least * (count - 1)
    while rest > 0:
        movable = [i for i in range(1, count) if holding[i] < largest] or [i for i in range(1, count) if holding[i] < reach]
        whole, budget = sum([portions[i] for i in movable]), rest
        for i in movable:
            more = min(reach - holding[i], max(1, budget * portions[i] // whole), rest)
            holding[i] = holding[i] + more
            rest = rest - more
    return np.array(holding)


def noise(stream_key, extent, width, bound, split=(), held_as=jnp.bfloat16):
    values = jax.random.normal(stream_key, extent, jnp.float32) * width
    if len(split) > 0:
        values = shard_levels(stream_key, extent, split, -0.22, 0.18) * values
    return jnp.clip(values, min=-bound, max=bound).astype(held_as)


def setup_inputs(seed: int = 0) -> dict:
    key_list = jax.random.split(jax.random.key(seed), 9)
    tokens = noise(key_list[0], (TOKENS, D), 1.0, 6.0, ((0, 8), (1, 4)))
    gate_weight = noise(key_list[1], (EXPERTS, D, FFW), D ** -0.5, 0.09375, ((0, 8), (1, 4)))
    up_weight = noise(key_list[2], (EXPERTS, D, FFW), D ** -0.5, 0.09375, ((0, 8), (1, 4)))
    down_weight = noise(key_list[3], (EXPERTS, FFW, D), FFW ** -0.5, 0.21875, ((0, 8), (2, 4)))
    routes_keys = jax.random.split(jax.random.fold_in(key_list[4], 1), TOKENS // TOK_DEV)
    routes_turns = jax.random.permutation(jax.random.fold_in(key_list[4], 3), TOKENS // TOK_DEV)
    routes = jax.vmap(lambda own, number: deal_out(jax.random.fold_in(key_list[4], 2), own, number, TOK_DEV, EXPERTS, TOPK, CAP, 2))(routes_keys, routes_turns).reshape((TOKENS, TOPK))
    gate_levels = touch_ends(jax.random.randint(key_list[5], (TOKENS, TOPK), 1, 256), jax.random.fold_in(key_list[5], 1), 1, 255).astype(jnp.int32)
    log_ratio = noise(key_list[6], (TOKENS,), 0.5, 3.0, ((0, 8),), jnp.float32)
    cotangent = noise(key_list[7], (TOKENS, D), 1.0, 6.0, ((0, 8), (1, 4)))
    return dict(tokens=tokens, gate_weight=gate_weight, up_weight=up_weight, down_weight=down_weight, routes=routes, gate_levels=gate_levels, log_ratio=log_ratio, cotangent=cotangent)


clip_ratio = 2.0


def expert_pass(operands):
    rows_in, rows_grad, w_gate, w_up, w_down = operands
    gate = jnp.dot(rows_in, w_gate, preferred_element_type=jnp.float32)
    upper = jnp.dot(rows_in, w_up, preferred_element_type=jnp.float32)
    activated = (jax.nn.silu(gate) * upper).astype(jnp.bfloat16)
    expert_out = jnp.dot(activated, w_down, preferred_element_type=jnp.float32).astype(jnp.bfloat16)
    hidden_grad = jnp.dot(rows_grad, w_down.T, preferred_element_type=jnp.float32)
    sigmoid_gate = jax.nn.sigmoid(gate)
    gate_back = (hidden_grad * upper * sigmoid_gate * (1.0 + gate * (1.0 - sigmoid_gate))).astype(jnp.bfloat16)
    up_back = (hidden_grad * gate * sigmoid_gate).astype(jnp.bfloat16)
    input_back = jnp.dot(gate_back, w_gate.T, preferred_element_type=jnp.float32)
    input_back = (input_back + jnp.dot(up_back, w_up.T, preferred_element_type=jnp.float32)).astype(jnp.bfloat16)
    return expert_out, input_back


def reference(tokens, gate_weight, up_weight, down_weight, routes, gate_levels, log_ratio, cotangent):
    block_picks = TOK_DEV * TOPK
    pick_ids = routes.reshape(N_EXPERT, block_picks)
    onehot_table = (pick_ids[:, :, None] == jnp.arange(EXPERTS, dtype=jnp.int32)[None, None, :]).astype(jnp.int32)
    earlier = jnp.cumsum(onehot_table, axis=1) - onehot_table
    position = jnp.sum(earlier * onehot_table, axis=2).reshape(-1)
    source = (jnp.arange(TOKENS * TOPK, dtype=jnp.int32) // block_picks).astype(jnp.int32)
    per_expert = N_EXPERT * CAP
    target = routes.reshape(-1) * per_expert + source * CAP + position
    levels = gate_levels.astype(jnp.float32)
    fractions = levels / jnp.sum(levels, axis=1, keepdims=True)
    ratio_weight = jnp.minimum(jnp.exp(log_ratio), clip_ratio)
    weighted = (ratio_weight[:, None] * cotangent.astype(jnp.float32)).astype(jnp.bfloat16)
    weighted_wide = weighted.astype(jnp.float32)[:, None, :]
    pick_grad = (fractions[:, :, None] * weighted_wide).astype(jnp.bfloat16).reshape(-1, D)
    rows_in = jnp.zeros((EXPERTS * per_expert, D), jnp.bfloat16).at[target].set(jnp.repeat(tokens, TOPK, axis=0))
    rows_grad = jnp.zeros((EXPERTS * per_expert, D), jnp.bfloat16).at[target].set(pick_grad)
    outputs, backs = lax.map(expert_pass, (rows_in.reshape(EXPERTS, per_expert, D), rows_grad.reshape(EXPERTS, per_expert, D), gate_weight, up_weight, down_weight))
    picked = outputs.reshape(-1, D)[target].reshape(TOKENS, TOPK, D).astype(jnp.float32)
    mixed_out = jnp.sum(fractions[:, :, None] * picked, axis=1).astype(jnp.bfloat16)
    gate_grad = jnp.sum(weighted_wide * picked, axis=2)
    back_picked = backs.reshape(-1, D)[target].reshape(TOKENS, TOPK, D).astype(jnp.float32)
    token_grad = jnp.sum(back_picked, axis=1).astype(jnp.bfloat16)
    return mixed_out, token_grad, gate_grad
```

```python
import functools
import jax
import jax.numpy as jnp
from jax import lax
from jax.experimental import pallas as pl
from jax.experimental.pallas import tpu as pltpu
from jax.sharding import PartitionSpec as P

EXPERTS = 64
TOPK = 8
CAP = 40
VMEM_BYTES = 50 * 1024 * 1024

clip_ratio = 2.0


def dot_nn(a, b):
    return lax.dot_general(a, b, (((1,), (0,)), ((), ())), preferred_element_type=jnp.float32)


def dot_nt(a, b):
    return lax.dot_general(a, b, (((1,), (1,)), ((), ())), preferred_element_type=jnp.float32)


def dot_tn(a, b):
    return lax.dot_general(a, b, (((0,), (0,)), ((), ())), preferred_element_type=jnp.float32)


def one_hot(slots_ref, rows):
    slots = slots_ref[0]
    return slots == lax.broadcasted_iota(jnp.int32, (rows, slots.shape[-1]), 0)


def whole(shape):
    return pl.BlockSpec(shape, lambda g, me: (0,) * len(shape))


def expert_block(shape, halves):
    count = len(halves)
    return pl.BlockSpec(
        (1,) + shape,
        lambda g, me: (2 * ((g // count) ^ me[0]) + (halves[0] + g % count), 0, 0),
    )


def partial_kernel(count, me, same, other, slots, w_gate, w_up, w_down,
                   self_a, self_b, send_a, keep_a, send_b, keep_b):
    step = pl.program_id(0)
    part, half = step // count, step % count
    tokens, width = same.shape
    rows = self_a.shape[1]
    hidden = w_gate.shape[2]
    pick = jnp.where(one_hot(slots, rows), 1.0, 0.0).astype(jnp.bfloat16)
    taken = dot_nn(pick[:, :tokens], same[...]) + dot_nn(pick[:, tokens:], other[...])
    taken = taken.astype(jnp.bfloat16)
    features = width // 2
    gate = dot_nn(taken[:, :features], w_gate[0]).astype(jnp.bfloat16)
    up = dot_nn(taken[:, :features], w_up[0]).astype(jnp.bfloat16)
    back = dot_nt(taken[:, features:], w_down[0]).astype(jnp.bfloat16)

    def put_a(ref, *where):
        ref[(*where, slice(None), pl.ds(0, hidden))] = gate
        ref[(*where, slice(None), pl.ds(hidden, hidden // 2))] = up[:, : hidden // 2]

    def put_b(ref, *where):
        ref[(*where, slice(None), pl.ds(0, hidden // 2))] = up[:, hidden // 2 :]
        ref[(*where, slice(None), pl.ds(hidden // 2, hidden))] = back

    @pl.when(part == 0)
    def _():
        put_a(self_a, half)
        put_b(self_b, half)

    @pl.when(part == 1)
    def _():
        put_a(send_a, 0, half)
        put_b(keep_b, half)

    @pl.when(part == 2)
    def _():
        put_a(keep_a, half)
        put_b(send_b, 0, half)

    @pl.when(part == 3)
    def _():
        put_a(send_a, 1, half)
        put_b(send_b, 1, half)


def partial_sums(me, same, other, slots, w_gate, w_up, w_down, halves):
    count = len(halves)
    features, hidden = w_gate.shape[1:]
    rows, cols = 2 * CAP, 3 * hidden // 2
    one = jax.ShapeDtypeStruct((count, rows, cols), jnp.bfloat16)
    two = jax.ShapeDtypeStruct((2, count, rows, cols), jnp.bfloat16)
    outs = (one, one, two, one, two, one)
    steps = 4 * count
    return pl.pallas_call(
        functools.partial(partial_kernel, count),
        grid_spec=pltpu.PrefetchScalarGridSpec(
            num_scalar_prefetch=1,
            grid=(steps,),
            in_specs=[
                whole(same.shape),
                whole(other.shape),
                expert_block(slots.shape[1:], halves),
                expert_block((features, hidden), halves),
                expert_block((features, hidden), halves),
                expert_block((hidden, features), halves),
            ],
            out_specs=[whole(o.shape) for o in outs],
        ),
        out_shape=outs,
        compiler_params=pltpu.CompilerParams(vmem_limit_bytes=VMEM_BYTES),
        cost_estimate=pl.CostEstimate(
            flops=steps * rows * 10 * features * hidden,
            bytes_accessed=steps * features * hidden * 6,
            transcendentals=0,
        ),
    )(me, same, other, slots, w_gate, w_up, w_down)


def middle_kernel(self_a, self_b, first_a, first_b, last_a, last_b, slots, share,
                  out_a, out_b, grad):
    count, rows, cols = self_a.shape
    hidden = 2 * cols // 3
    half = hidden // 2
    for h in range(count):
        def total(own, first, last, lo, size):
            cut = pl.ds(lo, size)
            return (
                own[h, :, cut].astype(jnp.float32)
                + first[0, h, :, cut].astype(jnp.float32)
                + last[h, :, cut].astype(jnp.float32)
            )
        hot = one_hot(slots.at[pl.ds(h, 1)], rows)
        fraction = jnp.sum(jnp.where(hot, share[h], 0.0), axis=1, keepdims=True)
        grads = jnp.zeros((rows, 1), jnp.float32)
        for side in range(2):
            lo = side * half
            gate = total(self_a, first_a, last_a, lo, half)
            if side == 0:
                up = total(self_a, first_a, last_a, hidden, half)
            else:
                up = total(self_b, first_b, last_b, 0, half)
            back = total(self_b, first_b, last_b, half + lo, half)
            sig = 1.0 / (1.0 + jnp.exp(-gate))
            silu = gate * sig
            act = silu * up
            grads = grads + jnp.sum(act * back, axis=1, keepdims=True)
            hidden_grad = back * fraction
            act_out = (act * fraction).astype(jnp.bfloat16)
            gate_out = (hidden_grad * up * sig * (1.0 + gate * (1.0 - sig))).astype(jnp.bfloat16)
            up_out = (hidden_grad * silu).astype(jnp.bfloat16)
            out_a[h, :, pl.ds(lo, half)] = act_out
            if side == 0:
                out_a[h, :, pl.ds(hidden, half)] = gate_out
            else:
                out_b[h, :, pl.ds(0, half)] = gate_out
            out_b[h, :, pl.ds(half + lo, half)] = up_out
        grad[h] = jnp.sum(jnp.where(hot, grads, 0.0), axis=0, keepdims=True)


def middle(self_a, self_b, first_a, first_b, last_a, last_b, slots, share):
    outs = (
        jax.ShapeDtypeStruct(self_a.shape, jnp.bfloat16),
        jax.ShapeDtypeStruct(self_b.shape, jnp.bfloat16),
        jax.ShapeDtypeStruct(share.shape, jnp.float32),
    )
    return pl.pallas_call(
        middle_kernel,
        out_shape=outs,
        in_specs=[pl.BlockSpec(memory_space=pltpu.VMEM)] * 8,
        out_specs=[pl.BlockSpec(memory_space=pltpu.VMEM)] * 3,
        compiler_params=pltpu.CompilerParams(vmem_limit_bytes=VMEM_BYTES),
        cost_estimate=pl.CostEstimate(
            flops=40 * self_a.size, bytes_accessed=14 * self_a.size, transcendentals=self_a.size
        ),
    )(self_a, self_b, first_a, first_b, last_a, last_b, slots, share)


def combine_kernel(count, me, *refs):
    lefts, rights = refs[0:4], refs[4:8]
    slots, w_gate, w_up, w_down, same, other, rows_in, hots, outs = refs[8:]
    step = pl.program_id(0)
    part, half = step // count, step % count
    rows, cols = rows_in.shape[0], lefts[0].shape[2]
    hidden = w_gate.shape[2]
    features = w_gate.shape[1]
    for v in range(4):
        @pl.when(part == v)
        def _():
            rows_in[:, pl.ds(0, cols)] = lefts[v][half]
            rows_in[:, pl.ds(cols, cols)] = rights[v][half]
    at = pl.ds(pl.multiple_of(step * rows, 16), rows)
    outs[at, pl.ds(0, features)] = dot_nn(rows_in[:, pl.ds(0, hidden)], w_down[0]).astype(jnp.bfloat16)
    outs[at, pl.ds(features, features)] = (
        dot_nt(rows_in[:, pl.ds(hidden, hidden)], w_gate[0])
        + dot_nt(rows_in[:, pl.ds(2 * hidden, hidden)], w_up[0])
    ).astype(jnp.bfloat16)
    hots[at, :] = jnp.where(one_hot(slots, rows), 1.0, 0.0).astype(jnp.bfloat16)

    @pl.when(step == pl.num_programs(0) - 1)
    def _():
        tokens, width = same.shape
        for ref, lo in ((same, 0), (other, tokens)):
            ref[...] = dot_tn(hots[:, pl.ds(lo, tokens)], outs[...]).astype(jnp.bfloat16)


def combine(me, lefts, rights, slots, w_gate, w_up, w_down, halves):
    count = len(halves)
    features, hidden = w_gate.shape[1:]
    rows = 2 * CAP
    tokens = slots.shape[2] // 2
    steps = 4 * count
    out = jax.ShapeDtypeStruct((tokens, 2 * features), jnp.bfloat16)
    return pl.pallas_call(
        functools.partial(combine_kernel, count),
        grid_spec=pltpu.PrefetchScalarGridSpec(
            num_scalar_prefetch=1,
            grid=(steps,),
            in_specs=[whole(a.shape) for a in (*lefts, *rights)]
            + [
                expert_block(slots.shape[1:], halves),
                expert_block((features, hidden), halves),
                expert_block((features, hidden), halves),
                expert_block((hidden, features), halves),
            ],
            out_specs=[whole(out.shape)] * 2,
            scratch_shapes=[
                pltpu.VMEM((rows, 3 * hidden), jnp.bfloat16),
                pltpu.VMEM((steps * rows, 2 * tokens), jnp.bfloat16),
                pltpu.VMEM((steps * rows, 2 * features), jnp.bfloat16),
            ],
        ),
        out_shape=(out, out),
        compiler_params=pltpu.CompilerParams(vmem_limit_bytes=VMEM_BYTES),
        cost_estimate=pl.CostEstimate(
            flops=steps * rows * 10 * features * hidden,
            bytes_accessed=steps * features * hidden * 6,
            transcendentals=0,
        ),
    )(me, *lefts, *rights, slots, w_gate, w_up, w_down)


def swap(value, axis, bits):
    count = lax.axis_size(axis)
    return lax.ppermute(value, axis, [(n, n ^ bits) for n in range(count)])


def grouped(tokens, gate_weight, up_weight, down_weight, routes, gate_levels, log_ratio, cotangent):
    block, features = tokens.shape
    per_device = gate_weight.shape[0]
    peers = lax.axis_size("expert")
    chips = peers // 2
    mine = lax.axis_index("expert")
    member = lax.axis_index("dp")
    me = member.astype(jnp.int32).reshape(1)

    ratio_weight = jnp.minimum(jnp.exp(log_ratio), clip_ratio)
    weighted = (ratio_weight[:, None] * cotangent.astype(jnp.float32)).astype(jnp.bfloat16)
    payload = jnp.concatenate([tokens, weighted], axis=1)
    sames = [payload] + [swap(payload, "expert", 2 * o) for o in range(1, chips)]
    others = [swap(p, "expert", 1) for p in sames]

    picks = lax.all_gather(jnp.stack([routes, gate_levels]), "expert")
    order = jnp.arange(peers, dtype=jnp.int32) ^ mine
    picks = picks[order]
    levels = picks[:, 1].astype(jnp.float32)
    fractions = levels / jnp.sum(levels, axis=2, keepdims=True)
    local = mine * per_device + jnp.arange(per_device, dtype=jnp.int32)
    named = picks[:, 0][None] == local[:, None, None, None]
    share = jnp.sum(jnp.where(named, fractions[None], 0.0), axis=3)
    chosen = jnp.any(named, axis=3)
    tri = (jnp.arange(block)[:, None] < jnp.arange(block)[None, :]).astype(jnp.bfloat16)
    place = jnp.einsum(
        "jst,tu->jsu", chosen.astype(jnp.bfloat16), tri, preferred_element_type=jnp.float32
    ).astype(jnp.int32)
    place = place + (jnp.arange(peers, dtype=jnp.int32) % 2 * CAP)[None, :, None]
    slots = jnp.where(chosen, place, -1).reshape(per_device, chips, 1, 2 * block)
    share = share.reshape(per_device, chips, 1, 2 * block)

    weights = (gate_weight, up_weight, down_weight)
    chunks = [(0, (0,))] + [(o, (0, 1)) for o in range(1, chips)] + [(0, (1,))]
    partials, grads, totals = [], {}, []
    for o, halves in chunks:
        slot = slots[:, o]
        self_a, self_b, send_a, keep_a, send_b, keep_b = partial_sums(
            me, sames[o], others[o], slot, *weights, halves
        )
        first_a, first_b = swap(send_a, "dp", 1), swap(send_b, "dp", 2)
        last_a = swap(keep_a + first_a[1], "dp", 2)
        last_b = swap(keep_b + first_b[1], "dp", 1)
        first = 2 * member + halves[0]
        own_slot = lax.dynamic_slice_in_dim(slot, first, len(halves), 0)
        own_share = lax.dynamic_slice_in_dim(share[:, o], first, len(halves), 0)
        a, b, grad = middle(
            self_a, self_b, first_a, first_b, last_a, last_b, own_slot, own_share
        )
        for n, h in enumerate(halves):
            grads[o, h] = grad[n]
        a_x, a_y, b_x, b_y = swap(a, "dp", 1), swap(a, "dp", 2), swap(b, "dp", 1), swap(b, "dp", 2)
        a_d, b_d = swap(a_y, "dp", 1), swap(b_x, "dp", 2)
        same, other = combine(
            me, (a, a_x, a_y, a_d), (b, b_x, b_y, b_d), slot, *weights, halves
        )
        both = same.astype(jnp.float32) + swap(other, "expert", 1).astype(jnp.float32)
        if o:
            both = swap(both.astype(jnp.bfloat16), "expert", 2 * o)
        totals.append(both)
    total = sum(t.astype(jnp.float32) for t in totals).astype(jnp.bfloat16)

    grad_all = jnp.stack([jnp.stack([grads[o, h] for o in range(chips)]) for h in range(2)])
    grad_all = lax.all_gather(grad_all.reshape(2, peers, block), ("expert", "dp"))
    grad_all = grad_all.reshape(peers, per_device, peers, block)
    place_of = (jnp.arange(peers)[:, None] ^ mine) == jnp.arange(peers)[None, :]
    to_me = jnp.sum(jnp.where(place_of[:, None, :, None], grad_all, 0.0), axis=2)
    to_me = to_me.reshape(peers * per_device, block)
    hit = routes[:, :, None] == jnp.arange(EXPERTS, dtype=jnp.int32)
    gate_grad = jnp.sum(jnp.where(hit, to_me.T[:, None, :], 0.0), axis=2)
    return total[:, :features], total[:, features:], gate_grad


def on_device(
    tokens, gate_weight, up_weight, down_weight, routes, gate_levels, log_ratio, cotangent
):
    local_tokens = tokens.shape[0]
    feature_slice = tokens.shape[1]
    hidden = gate_weight.shape[2]
    per_device = gate_weight.shape[0]
    peer_count = lax.axis_size("expert")
    slots_total = EXPERTS * CAP
    pick_ids = routes.reshape(-1)
    onehot_table = (pick_ids[:, None] == jnp.arange(EXPERTS, dtype=jnp.int32)[None, :]).astype(
        jnp.int32
    )
    earlier = jnp.cumsum(onehot_table, axis=0) - onehot_table
    position = jnp.sum(earlier * onehot_table, axis=1)
    target = pick_ids * CAP + position

    def pack_rows(values):
        packed = jnp.zeros((slots_total, feature_slice), jnp.bfloat16).at[target].set(values)
        return packed.reshape(peer_count, per_device * CAP, feature_slice)

    received = lax.all_to_all(
        pack_rows(jnp.repeat(tokens, TOPK, axis=0)),
        "expert",
        split_axis=0,
        concat_axis=0,
        tiled=True,
    )
    arrived = received.reshape(peer_count, per_device, CAP, feature_slice)
    gate_part = jnp.einsum(
        "sjcd,jdf->sjcf", arrived, gate_weight, preferred_element_type=jnp.float32
    ).reshape(-1, hidden)
    up_part = jnp.einsum(
        "sjcd,jdf->sjcf", arrived, up_weight, preferred_element_type=jnp.float32
    ).reshape(-1, hidden)
    gate_share, up_share = (
        lax.psum_scatter(gate_part, "dp", scatter_dimension=0, tiled=True),
        lax.psum_scatter(up_part, "dp", scatter_dimension=0, tiled=True),
    )
    activated = lax.all_gather(
        (jax.nn.silu(gate_share) * up_share).astype(jnp.bfloat16), "dp", axis=0, tiled=True
    )
    expert_out = jnp.einsum(
        "sjcf,jfd->sjcd",
        activated.reshape(peer_count, per_device, CAP, hidden),
        down_weight,
        preferred_element_type=jnp.float32,
    ).astype(jnp.bfloat16)
    returned = lax.all_to_all(
        expert_out.reshape(peer_count, per_device * CAP, feature_slice),
        "expert",
        split_axis=0,
        concat_axis=0,
        tiled=True,
    )
    picked = (
        returned.reshape(slots_total, feature_slice)[target]
        .reshape(local_tokens, TOPK, feature_slice)
        .astype(jnp.float32)
    )
    levels = gate_levels.astype(jnp.float32)
    fractions = levels / jnp.sum(levels, axis=1, keepdims=True)
    mixed_out = jnp.sum(fractions[:, :, None] * picked, axis=1).astype(jnp.bfloat16)
    ratio_weight = jnp.minimum(jnp.exp(log_ratio), clip_ratio)
    weighted = (ratio_weight[:, None] * cotangent.astype(jnp.float32)).astype(jnp.bfloat16)
    weighted_wide = weighted.astype(jnp.float32)[:, None, :]
    gate_grad = lax.psum(jnp.sum(weighted_wide * picked, axis=2), "dp")
    pick_grad = (
        (fractions[:, :, None] * weighted_wide).astype(jnp.bfloat16).reshape(-1, feature_slice)
    )
    back_rows = lax.all_to_all(
        pack_rows(pick_grad), "expert", split_axis=0, concat_axis=0, tiled=True
    )
    back_rows = back_rows.reshape(peer_count, per_device, CAP, feature_slice)
    hidden_part = jnp.einsum(
        "sjcd,jfd->sjcf", back_rows, down_weight, preferred_element_type=jnp.float32
    ).reshape(-1, hidden)
    hidden_grad = lax.psum_scatter(hidden_part, "dp", scatter_dimension=0, tiled=True)
    sigmoid_gate = jax.nn.sigmoid(gate_share)
    gate_back = (
        hidden_grad * up_share * sigmoid_gate * (1.0 + gate_share * (1.0 - sigmoid_gate))
    ).astype(jnp.bfloat16)
    up_back = (hidden_grad * gate_share * sigmoid_gate).astype(jnp.bfloat16)
    gate_rows, up_rows = (
        lax.all_gather(gate_back, "dp", axis=0, tiled=True),
        lax.all_gather(up_back, "dp", axis=0, tiled=True),
    )
    gate_rows = gate_rows.reshape(peer_count, per_device, CAP, hidden)
    up_rows = up_rows.reshape(peer_count, per_device, CAP, hidden)
    input_part = jnp.einsum(
        "sjcf,jdf->sjcd", gate_rows, gate_weight, preferred_element_type=jnp.float32
    )
    input_part = (
        input_part
        + jnp.einsum("sjcf,jdf->sjcd", up_rows, up_weight, preferred_element_type=jnp.float32)
    ).astype(jnp.bfloat16)
    input_back = lax.all_to_all(
        input_part.reshape(peer_count, per_device * CAP, feature_slice),
        "expert",
        split_axis=0,
        concat_axis=0,
        tiled=True,
    )
    back_picked = input_back.reshape(slots_total, feature_slice)[target].reshape(
        local_tokens, TOPK, feature_slice
    )
    token_grad = jnp.sum(back_picked.astype(jnp.float32), axis=1).astype(jnp.bfloat16)
    return (mixed_out, token_grad, gate_grad)


def solution(mesh):
    in_specs = (
        P("expert", "dp"),
        P("expert", "dp", None),
        P("expert", "dp", None),
        P("expert", None, "dp"),
        P("expert", None),
        P("expert", None),
        P("expert"),
        P("expert", "dp"),
    )
    out_specs = (P("expert", "dp"), P("expert", "dp"), P("expert", None))
    fits = mesh.shape["dp"] == 4 and mesh.shape["expert"] == 8
    return jax.shard_map(
        grouped if fits else on_device,
        mesh=mesh, in_specs=in_specs, out_specs=out_specs, check_vma=False,
    )
```

```python
import functools
import jax
import jax.numpy as jnp
from jax import lax
from jax.experimental import pallas as pl
from jax.experimental.pallas import tpu as pltpu
from jax.sharding import PartitionSpec as P

EXPERTS = 64
TOPK = 8
CAP = 40
VMEM_BYTES = 50 * 1024 * 1024

clip_ratio = 2.0


def dot_nn(a, b):
    return lax.dot_general(a, b, (((1,), (0,)), ((), ())), preferred_element_type=jnp.float32)


def dot_nt(a, b):
    return lax.dot_general(a, b, (((1,), (1,)), ((), ())), preferred_element_type=jnp.float32)


def dot_tn(a, b):
    return lax.dot_general(a, b, (((0,), (0,)), ((), ())), preferred_element_type=jnp.float32)


def one_hot(slots_ref, rows):
    slots = slots_ref[0]
    return slots == lax.broadcasted_iota(jnp.int32, (rows, slots.shape[-1]), 0)


def whole(shape):
    return pl.BlockSpec(shape, lambda g, me: (0,) * len(shape))


def expert_block(shape, halves):
    count = len(halves)
    return pl.BlockSpec(
        (1,) + shape,
        lambda g, me: (2 * ((g // count) ^ me[0]) + (halves[0] + g % count), 0, 0),
    )


def partial_kernel(count, me, same, other, slots, w_gate, w_up, w_down,
                   self_a, self_b, send_a, keep_a, send_b, keep_b):
    step = pl.program_id(0)
    part, half = step // count, step % count
    tokens, width = same.shape
    rows = self_a.shape[1]
    hidden = w_gate.shape[2]
    pick = jnp.where(one_hot(slots, rows), 1.0, 0.0).astype(jnp.bfloat16)
    taken = dot_nn(pick[:, :tokens], same[...]) + dot_nn(pick[:, tokens:], other[...])
    taken = taken.astype(jnp.bfloat16)
    features = width // 2
    gate = dot_nn(taken[:, :features], w_gate[0]).astype(jnp.bfloat16)
    up = dot_nn(taken[:, :features], w_up[0]).astype(jnp.bfloat16)
    back = dot_nt(taken[:, features:], w_down[0]).astype(jnp.bfloat16)

    def put_a(ref, *where):
        ref[(*where, slice(None), pl.ds(0, hidden))] = gate
        ref[(*where, slice(None), pl.ds(hidden, hidden // 2))] = up[:, : hidden // 2]

    def put_b(ref, *where):
        ref[(*where, slice(None), pl.ds(0, hidden // 2))] = up[:, hidden // 2 :]
        ref[(*where, slice(None), pl.ds(hidden // 2, hidden))] = back

    @pl.when(part == 0)
    def _():
        put_a(self_a, half)
        put_b(self_b, half)

    @pl.when(part == 1)
    def _():
        put_a(send_a, 0, half)
        put_b(keep_b, half)

    @pl.when(part == 2)
    def _():
        put_a(keep_a, half)
        put_b(send_b, 0, half)

    @pl.when(part == 3)
    def _():
        put_a(send_a, 1, half)
        put_b(send_b, 1, half)


def partial_sums(me, same, other, slots, w_gate, w_up, w_down, halves):
    count = len(halves)
    features, hidden = w_gate.shape[1:]
    rows, cols = 2 * CAP, 3 * hidden // 2
    one = jax.ShapeDtypeStruct((count, rows, cols), jnp.bfloat16)
    two = jax.ShapeDtypeStruct((2, count, rows, cols), jnp.bfloat16)
    outs = (one, one, two, one, two, one)
    steps = 4 * count
    return pl.pallas_call(
        functools.partial(partial_kernel, count),
        grid_spec=pltpu.PrefetchScalarGridSpec(
            num_scalar_prefetch=1,
            grid=(steps,),
            in_specs=[
                whole(same.shape),
                whole(other.shape),
                expert_block(slots.shape[1:], halves),
                expert_block((features, hidden), halves),
                expert_block((features, hidden), halves),
                expert_block((hidden, features), halves),
            ],
            out_specs=[whole(o.shape) for o in outs],
        ),
        out_shape=outs,
        compiler_params=pltpu.CompilerParams(vmem_limit_bytes=VMEM_BYTES),
        cost_estimate=pl.CostEstimate(
            flops=steps * rows * 10 * features * hidden,
            bytes_accessed=steps * features * hidden * 6,
            transcendentals=0,
        ),
    )(me, same, other, slots, w_gate, w_up, w_down)


def middle_kernel(me, self_a, self_b, first_a, first_b, last_a, last_b, slots, share,
                  out_a, out_b):
    count, rows, cols = self_a.shape
    hidden = 2 * cols // 3
    half = hidden // 2
    for h in range(count):
        def total(own, first, last, lo, size):
            cut = pl.ds(lo, size)
            return (
                own[h, :, cut].astype(jnp.float32)
                + first[0, h, :, cut].astype(jnp.float32)
                + last[h, :, cut].astype(jnp.float32)
            )
        hot = one_hot(slots.at[pl.ds(h, 1)], rows)
        fraction = jnp.sum(jnp.where(hot, share[h], 0.0), axis=1, keepdims=True)
        grads = jnp.zeros((rows, 1), jnp.float32)
        for side in range(2):
            lo = side * half
            gate = total(self_a, first_a, last_a, lo, half)
            if side == 0:
                up = total(self_a, first_a, last_a, hidden, half)
            else:
                up = total(self_b, first_b, last_b, 0, half)
            back = total(self_b, first_b, last_b, half + lo, half)
            sig = 1.0 / (1.0 + jnp.exp(-gate))
            silu = gate * sig
            act = silu * up
            grads = grads + jnp.sum(act * back, axis=1, keepdims=True)
            hidden_grad = back * fraction
            act_out = (act * fraction).astype(jnp.bfloat16)
            gate_out = (hidden_grad * up * sig * (1.0 + gate * (1.0 - sig))).astype(jnp.bfloat16)
            up_out = (hidden_grad * silu).astype(jnp.bfloat16)
            out_a[h, :, pl.ds(lo, half)] = act_out
            if side == 0:
                out_a[h, :, pl.ds(hidden, half)] = gate_out
            else:
                out_b[h, :, pl.ds(0, half)] = gate_out
            out_b[h, :, pl.ds(half + lo, half)] = up_out
        lane = lax.broadcasted_iota(jnp.int32, (rows, 2 * EXPERTS), 1)
        high = grads.astype(jnp.bfloat16).astype(jnp.float32)
        spread = jnp.where(lane == me[0] + h, high, 0.0)
        spread = jnp.where(lane == me[0] + h + EXPERTS, grads - high, spread)
        out_a[h, :, pl.ds(cols, 2 * EXPERTS)] = spread.astype(jnp.bfloat16)


def middle(first, self_a, self_b, first_a, first_b, last_a, last_b, slots, share):
    count, rows, cols = self_a.shape
    outs = (
        jax.ShapeDtypeStruct((count, rows, cols + 2 * EXPERTS), jnp.bfloat16),
        jax.ShapeDtypeStruct(self_b.shape, jnp.bfloat16),
    )
    return pl.pallas_call(
        middle_kernel,
        out_shape=outs,
        in_specs=[pl.BlockSpec(memory_space=pltpu.SMEM)]
        + [pl.BlockSpec(memory_space=pltpu.VMEM)] * 8,
        out_specs=[pl.BlockSpec(memory_space=pltpu.VMEM)] * 2,
        compiler_params=pltpu.CompilerParams(vmem_limit_bytes=VMEM_BYTES),
        cost_estimate=pl.CostEstimate(
            flops=40 * self_a.size, bytes_accessed=14 * self_a.size, transcendentals=self_a.size
        ),
    )(first, self_a, self_b, first_a, first_b, last_a, last_b, slots, share)


def combine_kernel(count, me, *refs):
    lefts, rights = refs[0:4], refs[4:8]
    slots, w_gate, w_up, w_down, same, other, rows_in, hots, outs = refs[8:]
    step = pl.program_id(0)
    part, half = step // count, step % count
    rows, cols = rows_in.shape[0], rights[0].shape[2]
    hidden = w_gate.shape[2]
    features = w_gate.shape[1]
    at = pl.ds(pl.multiple_of(step * rows, 16), rows)
    for v in range(4):
        @pl.when(part == v)
        def _():
            rows_in[:, pl.ds(0, cols)] = lefts[v][half, :, pl.ds(0, cols)]
            rows_in[:, pl.ds(cols, cols)] = rights[v][half]
            outs[at, pl.ds(2 * features, 2 * EXPERTS)] = lefts[v][half, :, pl.ds(cols, 2 * EXPERTS)]
    outs[at, pl.ds(0, features)] = dot_nn(rows_in[:, pl.ds(0, hidden)], w_down[0]).astype(jnp.bfloat16)
    outs[at, pl.ds(features, features)] = (
        dot_nt(rows_in[:, pl.ds(hidden, hidden)], w_gate[0])
        + dot_nt(rows_in[:, pl.ds(2 * hidden, hidden)], w_up[0])
    ).astype(jnp.bfloat16)
    hots[at, :] = jnp.where(one_hot(slots, rows), 1.0, 0.0).astype(jnp.bfloat16)

    @pl.when(step == pl.num_programs(0) - 1)
    def _():
        tokens, width = same.shape
        for ref, lo in ((same, 0), (other, tokens)):
            ref[...] = dot_tn(hots[:, pl.ds(lo, tokens)], outs[...]).astype(jnp.bfloat16)


def combine(me, lefts, rights, slots, w_gate, w_up, w_down, halves):
    count = len(halves)
    features, hidden = w_gate.shape[1:]
    rows = 2 * CAP
    tokens = slots.shape[2] // 2
    steps = 4 * count
    width = 2 * features + 2 * EXPERTS
    out = jax.ShapeDtypeStruct((tokens, width), jnp.bfloat16)
    return pl.pallas_call(
        functools.partial(combine_kernel, count),
        grid_spec=pltpu.PrefetchScalarGridSpec(
            num_scalar_prefetch=1,
            grid=(steps,),
            in_specs=[whole(a.shape) for a in (*lefts, *rights)]
            + [
                expert_block(slots.shape[1:], halves),
                expert_block((features, hidden), halves),
                expert_block((features, hidden), halves),
                expert_block((hidden, features), halves),
            ],
            out_specs=[whole(out.shape)] * 2,
            scratch_shapes=[
                pltpu.VMEM((rows, 3 * hidden), jnp.bfloat16),
                pltpu.VMEM((steps * rows, 2 * tokens), jnp.bfloat16),
                pltpu.VMEM((steps * rows, width), jnp.bfloat16),
            ],
        ),
        out_shape=(out, out),
        compiler_params=pltpu.CompilerParams(vmem_limit_bytes=VMEM_BYTES),
        cost_estimate=pl.CostEstimate(
            flops=steps * rows * 10 * features * hidden,
            bytes_accessed=steps * features * hidden * 6,
            transcendentals=0,
        ),
    )(me, *lefts, *rights, slots, w_gate, w_up, w_down)


def swap(value, axis, bits):
    count = lax.axis_size(axis)
    return lax.ppermute(value, axis, [(n, n ^ bits) for n in range(count)])


def grouped(tokens, gate_weight, up_weight, down_weight, routes, gate_levels, log_ratio, cotangent):
    block, features = tokens.shape
    per_device = gate_weight.shape[0]
    peers = lax.axis_size("expert")
    chips = peers // 2
    mine = lax.axis_index("expert")
    member = lax.axis_index("dp")
    me = member.astype(jnp.int32).reshape(1)

    ratio_weight = jnp.minimum(jnp.exp(log_ratio), clip_ratio)
    weighted = (ratio_weight[:, None] * cotangent.astype(jnp.float32)).astype(jnp.bfloat16)
    payload = jnp.concatenate([tokens, weighted], axis=1)
    sames = [payload] + [swap(payload, "expert", 2 * o) for o in range(1, chips)]
    others = [swap(p, "expert", 1) for p in sames]

    local = mine * per_device + jnp.arange(per_device, dtype=jnp.int32)
    tri = (jnp.arange(block)[:, None] < jnp.arange(block)[None, :]).astype(jnp.bfloat16)

    def placed(picks):
        levels = picks[:, 1].astype(jnp.float32)
        fractions = levels / jnp.sum(levels, axis=1, keepdims=True)
        named = picks[:, 0][None] == local[:, None, None, None]
        share = jnp.sum(jnp.where(named, fractions[None], 0.0), axis=2)
        chosen = jnp.any(named, axis=2)
        place = jnp.einsum(
            "jst,tu->jsu", chosen.astype(jnp.bfloat16), tri, preferred_element_type=jnp.float32
        ).astype(jnp.int32)
        place = place + (jnp.arange(picks.shape[0], dtype=jnp.int32) % 2 * CAP)[None, :, None]
        slots = jnp.where(chosen, place, -1)
        pairs = (per_device, picks.shape[0] // 2, 1, 2 * block)
        return slots.reshape(pairs), share.reshape(pairs)

    picks = jnp.stack([routes.T, gate_levels.T])
    near = jnp.stack([picks, swap(picks, "expert", 1)])
    away = jnp.stack([swap(picks, "expert", 2 * o) for o in range(1, chips)])
    far = jnp.stack([away, swap(away, "expert", 1)], axis=1).reshape(-1, *picks.shape)
    near_slots, near_share = placed(near)
    far_slots, far_share = placed(far)

    weights = (gate_weight, up_weight, down_weight)
    chunks = [(0, (0,))] + [(o, (0, 1)) for o in range(1, chips)] + [(0, (1,))]
    totals = []
    for o, halves in chunks:
        slot = far_slots[:, o - 1] if o else near_slots[:, 0]
        part = far_share[:, o - 1] if o else near_share[:, 0]
        self_a, self_b, send_a, keep_a, send_b, keep_b = partial_sums(
            me, sames[o], others[o], slot, *weights, halves
        )
        first_a, first_b = swap(send_a, "dp", 1), swap(send_b, "dp", 2)
        last_a = swap(keep_a + first_a[1], "dp", 2)
        last_b = swap(keep_b + first_b[1], "dp", 1)
        first = 2 * member + halves[0]
        own_slot = lax.dynamic_slice_in_dim(slot, first, len(halves), 0)
        own_share = lax.dynamic_slice_in_dim(part, first, len(halves), 0)
        expert = (mine * per_device + first).astype(jnp.int32).reshape(1)
        a, b = middle(
            expert, self_a, self_b, first_a, first_b, last_a, last_b, own_slot, own_share
        )
        a_x, a_y, b_x, b_y = swap(a, "dp", 1), swap(a, "dp", 2), swap(b, "dp", 1), swap(b, "dp", 2)
        a_d, b_d = swap(a_y, "dp", 1), swap(b_x, "dp", 2)
        same, other = combine(
            me, (a, a_x, a_y, a_d), (b, b_x, b_y, b_d), slot, *weights, halves
        )
        both = same.astype(jnp.float32) + swap(other, "expert", 1).astype(jnp.float32)
        if o:
            both = swap(both.astype(jnp.bfloat16), "expert", 2 * o)
        totals.append(both)
    total = sum(t.astype(jnp.float32) for t in totals)
    grads = total[:, 2 * features : 2 * features + EXPERTS] + total[:, 2 * features + EXPERTS :]
    hit = routes[:, :, None] == jnp.arange(EXPERTS, dtype=jnp.int32)
    gate_grad = jnp.sum(jnp.where(hit, grads[:, None, :], 0.0), axis=2)
    total = total[:, : 2 * features].astype(jnp.bfloat16)
    return total[:, :features], total[:, features:], gate_grad


def on_device(
    tokens, gate_weight, up_weight, down_weight, routes, gate_levels, log_ratio, cotangent
):
    local_tokens = tokens.shape[0]
    feature_slice = tokens.shape[1]
    hidden = gate_weight.shape[2]
    per_device = gate_weight.shape[0]
    peer_count = lax.axis_size("expert")
    slots_total = EXPERTS * CAP
    pick_ids = routes.reshape(-1)
    onehot_table = (pick_ids[:, None] == jnp.arange(EXPERTS, dtype=jnp.int32)[None, :]).astype(
        jnp.int32
    )
    earlier = jnp.cumsum(onehot_table, axis=0) - onehot_table
    position = jnp.sum(earlier * onehot_table, axis=1)
    target = pick_ids * CAP + position

    def pack_rows(values):
        packed = jnp.zeros((slots_total, feature_slice), jnp.bfloat16).at[target].set(values)
        return packed.reshape(peer_count, per_device * CAP, feature_slice)

    received = lax.all_to_all(
        pack_rows(jnp.repeat(tokens, TOPK, axis=0)),
        "expert",
        split_axis=0,
        concat_axis=0,
        tiled=True,
    )
    arrived = received.reshape(peer_count, per_device, CAP, feature_slice)
    gate_part = jnp.einsum(
        "sjcd,jdf->sjcf", arrived, gate_weight, preferred_element_type=jnp.float32
    ).reshape(-1, hidden)
    up_part = jnp.einsum(
        "sjcd,jdf->sjcf", arrived, up_weight, preferred_element_type=jnp.float32
    ).reshape(-1, hidden)
    gate_share, up_share = (
        lax.psum_scatter(gate_part, "dp", scatter_dimension=0, tiled=True),
        lax.psum_scatter(up_part, "dp", scatter_dimension=0, tiled=True),
    )
    activated = lax.all_gather(
        (jax.nn.silu(gate_share) * up_share).astype(jnp.bfloat16), "dp", axis=0, tiled=True
    )
    expert_out = jnp.einsum(
        "sjcf,jfd->sjcd",
        activated.reshape(peer_count, per_device, CAP, hidden),
        down_weight,
        preferred_element_type=jnp.float32,
    ).astype(jnp.bfloat16)
    returned = lax.all_to_all(
        expert_out.reshape(peer_count, per_device * CAP, feature_slice),
        "expert",
        split_axis=0,
        concat_axis=0,
        tiled=True,
    )
    picked = (
        returned.reshape(slots_total, feature_slice)[target]
        .reshape(local_tokens, TOPK, feature_slice)
        .astype(jnp.float32)
    )
    levels = gate_levels.astype(jnp.float32)
    fractions = levels / jnp.sum(levels, axis=1, keepdims=True)
    mixed_out = jnp.sum(fractions[:, :, None] * picked, axis=1).astype(jnp.bfloat16)
    ratio_weight = jnp.minimum(jnp.exp(log_ratio), clip_ratio)
    weighted = (ratio_weight[:, None] * cotangent.astype(jnp.float32)).astype(jnp.bfloat16)
    weighted_wide = weighted.astype(jnp.float32)[:, None, :]
    gate_grad = lax.psum(jnp.sum(weighted_wide * picked, axis=2), "dp")
    pick_grad = (
        (fractions[:, :, None] * weighted_wide).astype(jnp.bfloat16).reshape(-1, feature_slice)
    )
    back_rows = lax.all_to_all(
        pack_rows(pick_grad), "expert", split_axis=0, concat_axis=0, tiled=True
    )
    back_rows = back_rows.reshape(peer_count, per_device, CAP, feature_slice)
    hidden_part = jnp.einsum(
        "sjcd,jfd->sjcf", back_rows, down_weight, preferred_element_type=jnp.float32
    ).reshape(-1, hidden)
    hidden_grad = lax.psum_scatter(hidden_part, "dp", scatter_dimension=0, tiled=True)
    sigmoid_gate = jax.nn.sigmoid(gate_share)
    gate_back = (
        hidden_grad * up_share * sigmoid_gate * (1.0 + gate_share * (1.0 - sigmoid_gate))
    ).astype(jnp.bfloat16)
    up_back = (hidden_grad * gate_share * sigmoid_gate).astype(jnp.bfloat16)
    gate_rows, up_rows = (
        lax.all_gather(gate_back, "dp", axis=0, tiled=True),
        lax.all_gather(up_back, "dp", axis=0, tiled=True),
    )
    gate_rows = gate_rows.reshape(peer_count, per_device, CAP, hidden)
    up_rows = up_rows.reshape(peer_count, per_device, CAP, hidden)
    input_part = jnp.einsum(
        "sjcf,jdf->sjcd", gate_rows, gate_weight, preferred_element_type=jnp.float32
    )
    input_part = (
        input_part
        + jnp.einsum("sjcf,jdf->sjcd", up_rows, up_weight, preferred_element_type=jnp.float32)
    ).astype(jnp.bfloat16)
    input_back = lax.all_to_all(
        input_part.reshape(peer_count, per_device * CAP, feature_slice),
        "expert",
        split_axis=0,
        concat_axis=0,
        tiled=True,
    )
    back_picked = input_back.reshape(slots_total, feature_slice)[target].reshape(
        local_tokens, TOPK, feature_slice
    )
    token_grad = jnp.sum(back_picked.astype(jnp.float32), axis=1).astype(jnp.bfloat16)
    return (mixed_out, token_grad, gate_grad)


def solution(mesh):
    in_specs = (
        P("expert", "dp"),
        P("expert", "dp", None),
        P("expert", "dp", None),
        P("expert", None, "dp"),
        P("expert", None),
        P("expert", None),
        P("expert"),
        P("expert", "dp"),
    )
    out_specs = (P("expert", "dp"), P("expert", "dp"), P("expert", None))
    fits = mesh.shape["dp"] == 4 and mesh.shape["expert"] == 8
    return jax.shard_map(
        grouped if fits else on_device,
        mesh=mesh, in_specs=in_specs, out_specs=out_specs, check_vma=False,
    )
```

```python
import functools
import jax
import jax.numpy as jnp
from jax import lax
from jax.experimental import pallas as pl
from jax.experimental.pallas import tpu as pltpu
from jax.sharding import PartitionSpec as P

EXPERTS = 64
TOPK = 8
CAP = 40
VMEM_BYTES = 50 * 1024 * 1024

clip_ratio = 2.0


def dot_nn(a, b):
    return lax.dot_general(a, b, (((1,), (0,)), ((), ())), preferred_element_type=jnp.float32)


def dot_nt(a, b):
    return lax.dot_general(a, b, (((1,), (1,)), ((), ())), preferred_element_type=jnp.float32)


def dot_tn(a, b):
    return lax.dot_general(a, b, (((0,), (0,)), ((), ())), preferred_element_type=jnp.float32)


def one_hot(slots_ref, rows):
    slots = slots_ref[0]
    return slots == lax.broadcasted_iota(jnp.int32, (rows, slots.shape[-1]), 0)


def whole(shape):
    return pl.BlockSpec(shape, lambda g, me: (0,) * len(shape))


def expert_block(shape, halves):
    count = len(halves)
    return pl.BlockSpec(
        (1,) + shape,
        lambda g, me: (2 * ((g // count) ^ me[0]) + (halves[0] + g % count), 0, 0),
    )


def partial_kernel(count, me, same, other, slots, w_gate, w_up, w_down, after,
                   self_a, self_b, send_a, keep_a, send_b, keep_b):
    step = pl.program_id(0)
    part, half = step // count, step % count
    tokens, width = same.shape
    rows = self_a.shape[1]
    hidden = w_gate.shape[2]
    pick = jnp.where(one_hot(slots, rows), 1.0, 0.0).astype(jnp.bfloat16)
    taken = dot_nn(pick[:, :tokens], same[...]) + dot_nn(pick[:, tokens:], other[...])
    taken = taken.astype(jnp.bfloat16)
    features = width // 2
    gate = dot_nn(taken[:, :features], w_gate[0]).astype(jnp.bfloat16)
    up = dot_nn(taken[:, :features], w_up[0]).astype(jnp.bfloat16)
    back = dot_nt(taken[:, features:], w_down[0]).astype(jnp.bfloat16)

    def put_a(ref, *where):
        ref[(*where, slice(None), pl.ds(0, hidden))] = gate
        ref[(*where, slice(None), pl.ds(hidden, hidden // 2))] = up[:, : hidden // 2]

    def put_b(ref, *where):
        ref[(*where, slice(None), pl.ds(0, hidden // 2))] = up[:, hidden // 2 :]
        ref[(*where, slice(None), pl.ds(hidden // 2, hidden))] = back

    @pl.when(part == 0)
    def _():
        put_a(self_a, half)
        put_b(self_b, half)

    @pl.when(part == 1)
    def _():
        put_a(send_a, 0, half)
        put_b(keep_b, half)

    @pl.when(part == 2)
    def _():
        put_a(keep_a, half)
        put_b(send_b, 0, half)

    @pl.when(part == 3)
    def _():
        put_a(send_a, 1, half)
        put_b(send_b, 1, half)


def partial_sums(me, same, other, slots, w_gate, w_up, w_down, after, halves):
    count = len(halves)
    features, hidden = w_gate.shape[1:]
    rows, cols = 2 * CAP, 3 * hidden // 2
    one = jax.ShapeDtypeStruct((count, rows, cols), jnp.bfloat16)
    two = jax.ShapeDtypeStruct((2, count, rows, cols), jnp.bfloat16)
    outs = (one, one, two, one, two, one)
    steps = 4 * count
    return pl.pallas_call(
        functools.partial(partial_kernel, count),
        grid_spec=pltpu.PrefetchScalarGridSpec(
            num_scalar_prefetch=1,
            grid=(steps,),
            in_specs=[
                whole(same.shape),
                whole(other.shape),
                expert_block(slots.shape[1:], halves),
                expert_block((features, hidden), halves),
                expert_block((features, hidden), halves),
                expert_block((hidden, features), halves),
                pl.BlockSpec(memory_space=pl.ANY),
            ],
            out_specs=[whole(o.shape) for o in outs],
        ),
        out_shape=outs,
        compiler_params=pltpu.CompilerParams(vmem_limit_bytes=VMEM_BYTES),
        cost_estimate=pl.CostEstimate(
            flops=steps * rows * 10 * features * hidden,
            bytes_accessed=steps * features * hidden * 11,
            transcendentals=0,
        ),
    )(me, same, other, slots, w_gate, w_up, w_down, after)


def middle_kernel(me, self_a, self_b, first_a, first_b, last_a, last_b, slots, share, after, out):
    count, rows, cols = self_a.shape
    hidden = 2 * cols // 3
    half = hidden // 2
    extra = 2 * EXPERTS
    for h in range(count):
        def total(own, first, last, lo, size):
            cut = pl.ds(lo, size)
            return (
                own[h, :, cut].astype(jnp.float32)
                + first[0, h, :, cut].astype(jnp.float32)
                + last[h, :, cut].astype(jnp.float32)
            )
        hot = one_hot(slots.at[pl.ds(h, 1)], rows)
        fraction = jnp.sum(jnp.where(hot, share[h], 0.0), axis=1, keepdims=True)
        grads = jnp.zeros((rows, 1), jnp.float32)
        for side in range(2):
            lo = side * half
            gate = total(self_a, first_a, last_a, lo, half)
            if side == 0:
                up = total(self_a, first_a, last_a, hidden, half)
            else:
                up = total(self_b, first_b, last_b, 0, half)
            back = total(self_b, first_b, last_b, half + lo, half)
            sig = 1.0 / (1.0 + jnp.exp(-gate))
            silu = gate * sig
            act = silu * up
            grads = grads + jnp.sum(act * back, axis=1, keepdims=True)
            hidden_grad = back * fraction
            act_out = (act * fraction).astype(jnp.bfloat16)
            gate_out = (hidden_grad * up * sig * (1.0 + gate * (1.0 - sig))).astype(jnp.bfloat16)
            up_out = (hidden_grad * silu).astype(jnp.bfloat16)
            out[h, :, pl.ds(lo, half)] = act_out
            out[h, :, pl.ds(hidden + side * (half + extra), half)] = gate_out
            out[h, :, pl.ds(2 * hidden + extra + lo, half)] = up_out
        lane = lax.broadcasted_iota(jnp.int32, (rows, extra), 1)
        high = grads.astype(jnp.bfloat16).astype(jnp.float32)
        spread = jnp.where(lane == me[0] + h, high, 0.0)
        spread = jnp.where(lane == me[0] + h + EXPERTS, grads - high, spread)
        out[h, :, pl.ds(cols, extra)] = spread.astype(jnp.bfloat16)


def first_of(shape, at):
    return pl.BlockSpec((1,) + shape[1:], lambda g: (at,) + (0,) * (len(shape) - 1))


def at_once(shape):
    return pl.BlockSpec(shape, lambda g: (0,) * len(shape))


def middle(first, self_a, self_b, first_a, first_b, last_a, last_b, slots, share, after):
    count, rows, cols = self_a.shape
    out = jax.ShapeDtypeStruct((count, rows, 2 * cols + 2 * EXPERTS), jnp.bfloat16)
    return pl.pallas_call(
        middle_kernel,
        grid=(1,),
        out_shape=out,
        in_specs=[
            pl.BlockSpec(memory_space=pltpu.SMEM),
            at_once(self_a.shape),
            at_once(self_b.shape),
            first_of(first_a.shape, 0),
            first_of(first_b.shape, 0),
            at_once(last_a.shape),
            at_once(last_b.shape),
            at_once(slots.shape),
            at_once(share.shape),
            pl.BlockSpec(memory_space=pl.ANY),
        ],
        out_specs=at_once(out.shape),
        compiler_params=pltpu.CompilerParams(vmem_limit_bytes=VMEM_BYTES),
        cost_estimate=pl.CostEstimate(
            flops=40 * self_a.size, bytes_accessed=20 * self_a.size, transcendentals=self_a.size
        ),
    )(first, self_a, self_b, first_a, first_b, last_a, last_b, slots, share, after)


def between_kernel(adds, relays, *refs):
    ins, outs = refs[: 4 * adds + 2 * relays], refs[4 * adds + 2 * relays + 1 :]
    if adds:
        for n in range(2):
            outs[n][...] = (
                ins[n][...].astype(jnp.float32) + ins[2 + n][0].astype(jnp.float32)
            ).astype(jnp.bfloat16)
    if relays:
        rows_x, rows_y = ins[4 * adds :]
        out_a, out_b = outs[2 * adds :]
        cut = out_a.shape[2]
        out_a[...] = rows_y[:, :, pl.ds(0, cut)]
        out_b[...] = rows_x[:, :, pl.ds(cut, out_b.shape[2])]


def between(add, relay, after):
    ins, specs, outs = [], [], []
    if add is not None:
        keep_a, keep_b, first_a, first_b = add
        ins += [keep_a, keep_b, first_a, first_b]
        specs += [at_once(keep_a.shape), at_once(keep_b.shape)]
        specs += [first_of(first_a.shape, 1), first_of(first_b.shape, 1)]
        outs += [keep_a.shape, keep_b.shape]
    if relay is not None:
        ins += list(relay)
        specs += [at_once(r.shape) for r in relay]
        count, rows, width = relay[0].shape
        cols = (width - 2 * EXPERTS) // 2
        outs += [(count, rows, cols + 2 * EXPERTS), (count, rows, cols)]
    size = sum(i.size for i in ins)
    return pl.pallas_call(
        functools.partial(between_kernel, int(add is not None), int(relay is not None)),
        grid=(1,),
        out_shape=[jax.ShapeDtypeStruct(o, jnp.bfloat16) for o in outs],
        in_specs=specs + [pl.BlockSpec(memory_space=pl.ANY)],
        out_specs=[at_once(o) for o in outs],
        compiler_params=pltpu.CompilerParams(vmem_limit_bytes=VMEM_BYTES),
        cost_estimate=pl.CostEstimate(flops=size, bytes_accessed=4 * size, transcendentals=0),
    )(*ins, after)


def combine_kernel(count, me, *refs):
    across_a, across_b = refs[3:5]
    slots, w_gate, w_up, w_down, _, same, other, rows_in, hots, outs = refs[5:]
    step = pl.program_id(0)
    part, half = step // count, step % count
    rows, cols = rows_in.shape[0], across_b.shape[2]
    extra = pl.ds(cols, 2 * EXPERTS)
    hidden = w_gate.shape[2]
    features = w_gate.shape[1]
    at = pl.ds(pl.multiple_of(step * rows, 16), rows)
    for v in range(4):
        @pl.when(part == v)
        def _():
            left = refs[v] if v < 3 else across_a
            rows_in[:, pl.ds(0, cols)] = left[half, :, pl.ds(0, cols)]
            outs[at, pl.ds(2 * features, 2 * EXPERTS)] = left[half, :, extra]
            if v < 3:
                rows_in[:, pl.ds(cols, cols)] = left[half, :, pl.ds(cols + 2 * EXPERTS, cols)]
            else:
                rows_in[:, pl.ds(cols, cols)] = across_b[half]
    outs[at, pl.ds(0, features)] = dot_nn(rows_in[:, pl.ds(0, hidden)], w_down[0]).astype(jnp.bfloat16)
    outs[at, pl.ds(features, features)] = (
        dot_nt(rows_in[:, pl.ds(hidden, hidden)], w_gate[0])
        + dot_nt(rows_in[:, pl.ds(2 * hidden, hidden)], w_up[0])
    ).astype(jnp.bfloat16)
    hots[at, :] = jnp.where(one_hot(slots, rows), 1.0, 0.0).astype(jnp.bfloat16)

    @pl.when(step == pl.num_programs(0) - 1)
    def _():
        tokens, width = same.shape
        for ref, lo in ((same, 0), (other, tokens)):
            ref[...] = dot_tn(hots[:, pl.ds(lo, tokens)], outs[...]).astype(jnp.bfloat16)


def combine(me, given, slots, w_gate, w_up, w_down, after, halves):
    count = len(halves)
    features, hidden = w_gate.shape[1:]
    rows = 2 * CAP
    tokens = slots.shape[2] // 2
    steps = 4 * count
    width = 2 * features + 2 * EXPERTS
    out = jax.ShapeDtypeStruct((tokens, width), jnp.bfloat16)
    return pl.pallas_call(
        functools.partial(combine_kernel, count),
        grid_spec=pltpu.PrefetchScalarGridSpec(
            num_scalar_prefetch=1,
            grid=(steps,),
            in_specs=[whole(a.shape) for a in given]
            + [
                expert_block(slots.shape[1:], halves),
                expert_block((features, hidden), halves),
                expert_block((features, hidden), halves),
                expert_block((hidden, features), halves),
                pl.BlockSpec(memory_space=pl.ANY),
            ],
            out_specs=[whole(out.shape)] * 2,
            scratch_shapes=[
                pltpu.VMEM((rows, 3 * hidden), jnp.bfloat16),
                pltpu.VMEM((steps * rows, 2 * tokens), jnp.bfloat16),
                pltpu.VMEM((steps * rows, width), jnp.bfloat16),
            ],
        ),
        out_shape=(out, out),
        compiler_params=pltpu.CompilerParams(vmem_limit_bytes=VMEM_BYTES),
        cost_estimate=pl.CostEstimate(
            flops=steps * rows * 10 * features * hidden,
            bytes_accessed=steps * features * hidden * 11,
            transcendentals=0,
        ),
    )(me, *given, slots, w_gate, w_up, w_down, after)


def swap(value, axis, bits):
    count = lax.axis_size(axis)
    return lax.ppermute(value, axis, [(n, n ^ bits) for n in range(count)])


def grouped(tokens, gate_weight, up_weight, down_weight, routes, gate_levels, log_ratio, cotangent):
    block, features = tokens.shape
    per_device = gate_weight.shape[0]
    peers = lax.axis_size("expert")
    chips = peers // 2
    mine = lax.axis_index("expert")
    member = lax.axis_index("dp")
    me = member.astype(jnp.int32).reshape(1)

    ratio_weight = jnp.minimum(jnp.exp(log_ratio), clip_ratio)
    weighted = (ratio_weight[:, None] * cotangent.astype(jnp.float32)).astype(jnp.bfloat16)
    payload = jnp.concatenate([tokens, weighted], axis=1)
    across = swap(payload, "expert", 4)
    sames = [payload, swap(payload, "expert", 2), across, swap(across, "expert", 2)]
    others = [swap(p, "expert", 1) for p in sames]

    local = mine * per_device + jnp.arange(per_device, dtype=jnp.int32)
    tri = (jnp.arange(block)[:, None] < jnp.arange(block)[None, :]).astype(jnp.bfloat16)

    def placed(picks):
        levels = picks[:, 1].astype(jnp.float32)
        fractions = levels / jnp.sum(levels, axis=1, keepdims=True)
        named = picks[:, 0][None] == local[:, None, None, None]
        share = jnp.sum(jnp.where(named, fractions[None], 0.0), axis=2)
        chosen = jnp.any(named, axis=2)
        place = jnp.einsum(
            "jst,tu->jsu", chosen.astype(jnp.bfloat16), tri, preferred_element_type=jnp.float32
        ).astype(jnp.int32)
        place = place + (jnp.arange(picks.shape[0], dtype=jnp.int32) % 2 * CAP)[None, :, None]
        slots = jnp.where(chosen, place, -1)
        pairs = (per_device, picks.shape[0] // 2, 1, 2 * block)
        return slots.reshape(pairs), share.reshape(pairs)

    picks = jnp.stack([routes.T, gate_levels.T])
    near = jnp.stack([picks, swap(picks, "expert", 1)])
    away = jnp.stack([swap(picks, "expert", 2 * o) for o in range(1, chips)])
    far = jnp.stack([away, swap(away, "expert", 1)], axis=1).reshape(-1, *picks.shape)
    near_slots, near_share = placed(near)
    far_slots, far_share = placed(far)

    weights = (gate_weight, up_weight, down_weight)
    chunks = [(0, (0,)), (2, (0, 1)), (3, (0, 1)), (1, (0, 1)), (0, (1,))]
    count = len(chunks)
    sums, adds, sent, got, relayed, totals = {}, {}, {}, {}, {}, []
    after = near_slots

    def slots_of(k):
        o = chunks[k][0]
        return far_slots[:, o - 1] if o else near_slots[:, 0]

    def share_of(k):
        o = chunks[k][0]
        return far_share[:, o - 1] if o else near_share[:, 0]

    def start_rows(k, after):
        o, halves = chunks[k]
        out = partial_sums(me, sames[o], others[o], slots_of(k), *weights, after, halves)
        self_a, self_b, send_a, keep_a, send_b, keep_b = out
        firsts = swap(send_a, "dp", 1), swap(send_b, "dp", 2)
        sums[k] = self_a, self_b, *firsts
        adds[k] = keep_a, keep_b, *firsts
        return self_a

    def move(k, r, after):
        outs = between(adds.get(k), got.get(r), after)
        if k in adds:
            last_a, last_b = swap(outs[0], "dp", 2), swap(outs[1], "dp", 1)
            sums[k] = (*sums[k], last_a, last_b)
        if r in got:
            relayed[r] = swap(outs[-2], "dp", 1), swap(outs[-1], "dp", 2)
        return outs[0]

    def turn_rows(k, after):
        halves = chunks[k][1]
        first = 2 * member + halves[0]
        own_slot = lax.dynamic_slice_in_dim(slots_of(k), first, len(halves), 0)
        own_share = lax.dynamic_slice_in_dim(share_of(k), first, len(halves), 0)
        expert = (mine * per_device + first).astype(jnp.int32).reshape(1)
        sent[k] = middle(expert, *sums[k], own_slot, own_share, after)
        got[k] = swap(sent[k], "dp", 1), swap(sent[k], "dp", 2)
        return sent[k]

    def finish_rows(k, after):
        o, halves = chunks[k]
        given = (sent[k], *got[k], *relayed[k])
        same, other = combine(me, given, slots_of(k), *weights, after, halves)
        both = same.astype(jnp.float32) + swap(other, "expert", 1).astype(jnp.float32)
        if o:
            both = swap(both.astype(jnp.bfloat16), "expert", 2 * o)
        totals.append(both)
        return same

    after = start_rows(0, after)
    after = move(0, None, after)
    after = turn_rows(0, after)
    after = move(None, 0, after)
    for k in range(1, count):
        after = start_rows(k, after)
        if k == 1:
            after = finish_rows(0, after)
        else:
            after = turn_rows(k - 1, after)
            if k > 2:
                after = finish_rows(k - 2, after)
        after = move(k, k - 1 if k > 1 else None, after)
    after = turn_rows(count - 1, after)
    after = finish_rows(count - 2, after)
    after = move(None, count - 1, after)
    after = finish_rows(count - 1, after)
    total = sum(t.astype(jnp.float32) for t in totals)
    grads = total[:, 2 * features : 2 * features + EXPERTS] + total[:, 2 * features + EXPERTS :]
    hit = routes[:, :, None] == jnp.arange(EXPERTS, dtype=jnp.int32)
    gate_grad = jnp.sum(jnp.where(hit, grads[:, None, :], 0.0), axis=2)
    total = total[:, : 2 * features].astype(jnp.bfloat16)
    return total[:, :features], total[:, features:], gate_grad


def on_device(
    tokens, gate_weight, up_weight, down_weight, routes, gate_levels, log_ratio, cotangent
):
    local_tokens = tokens.shape[0]
    feature_slice = tokens.shape[1]
    hidden = gate_weight.shape[2]
    per_device = gate_weight.shape[0]
    peer_count = lax.axis_size("expert")
    slots_total = EXPERTS * CAP
    pick_ids = routes.reshape(-1)
    onehot_table = (pick_ids[:, None] == jnp.arange(EXPERTS, dtype=jnp.int32)[None, :]).astype(
        jnp.int32
    )
    earlier = jnp.cumsum(onehot_table, axis=0) - onehot_table
    position = jnp.sum(earlier * onehot_table, axis=1)
    target = pick_ids * CAP + position

    def pack_rows(values):
        packed = jnp.zeros((slots_total, feature_slice), jnp.bfloat16).at[target].set(values)
        return packed.reshape(peer_count, per_device * CAP, feature_slice)

    received = lax.all_to_all(
        pack_rows(jnp.repeat(tokens, TOPK, axis=0)),
        "expert",
        split_axis=0,
        concat_axis=0,
        tiled=True,
    )
    arrived = received.reshape(peer_count, per_device, CAP, feature_slice)
    gate_part = jnp.einsum(
        "sjcd,jdf->sjcf", arrived, gate_weight, preferred_element_type=jnp.float32
    ).reshape(-1, hidden)
    up_part = jnp.einsum(
        "sjcd,jdf->sjcf", arrived, up_weight, preferred_element_type=jnp.float32
    ).reshape(-1, hidden)
    gate_share, up_share = (
        lax.psum_scatter(gate_part, "dp", scatter_dimension=0, tiled=True),
        lax.psum_scatter(up_part, "dp", scatter_dimension=0, tiled=True),
    )
    activated = lax.all_gather(
        (jax.nn.silu(gate_share) * up_share).astype(jnp.bfloat16), "dp", axis=0, tiled=True
    )
    expert_out = jnp.einsum(
        "sjcf,jfd->sjcd",
        activated.reshape(peer_count, per_device, CAP, hidden),
        down_weight,
        preferred_element_type=jnp.float32,
    ).astype(jnp.bfloat16)
    returned = lax.all_to_all(
        expert_out.reshape(peer_count, per_device * CAP, feature_slice),
        "expert",
        split_axis=0,
        concat_axis=0,
        tiled=True,
    )
    picked = (
        returned.reshape(slots_total, feature_slice)[target]
        .reshape(local_tokens, TOPK, feature_slice)
        .astype(jnp.float32)
    )
    levels = gate_levels.astype(jnp.float32)
    fractions = levels / jnp.sum(levels, axis=1, keepdims=True)
    mixed_out = jnp.sum(fractions[:, :, None] * picked, axis=1).astype(jnp.bfloat16)
    ratio_weight = jnp.minimum(jnp.exp(log_ratio), clip_ratio)
    weighted = (ratio_weight[:, None] * cotangent.astype(jnp.float32)).astype(jnp.bfloat16)
    weighted_wide = weighted.astype(jnp.float32)[:, None, :]
    gate_grad = lax.psum(jnp.sum(weighted_wide * picked, axis=2), "dp")
    pick_grad = (
        (fractions[:, :, None] * weighted_wide).astype(jnp.bfloat16).reshape(-1, feature_slice)
    )
    back_rows = lax.all_to_all(
        pack_rows(pick_grad), "expert", split_axis=0, concat_axis=0, tiled=True
    )
    back_rows = back_rows.reshape(peer_count, per_device, CAP, feature_slice)
    hidden_part = jnp.einsum(
        "sjcd,jfd->sjcf", back_rows, down_weight, preferred_element_type=jnp.float32
    ).reshape(-1, hidden)
    hidden_grad = lax.psum_scatter(hidden_part, "dp", scatter_dimension=0, tiled=True)
    sigmoid_gate = jax.nn.sigmoid(gate_share)
    gate_back = (
        hidden_grad * up_share * sigmoid_gate * (1.0 + gate_share * (1.0 - sigmoid_gate))
    ).astype(jnp.bfloat16)
    up_back = (hidden_grad * gate_share * sigmoid_gate).astype(jnp.bfloat16)
    gate_rows, up_rows = (
        lax.all_gather(gate_back, "dp", axis=0, tiled=True),
        lax.all_gather(up_back, "dp", axis=0, tiled=True),
    )
    gate_rows = gate_rows.reshape(peer_count, per_device, CAP, hidden)
    up_rows = up_rows.reshape(peer_count, per_device, CAP, hidden)
    input_part = jnp.einsum(
        "sjcf,jdf->sjcd", gate_rows, gate_weight, preferred_element_type=jnp.float32
    )
    input_part = (
        input_part
        + jnp.einsum("sjcf,jdf->sjcd", up_rows, up_weight, preferred_element_type=jnp.float32)
    ).astype(jnp.bfloat16)
    input_back = lax.all_to_all(
        input_part.reshape(peer_count, per_device * CAP, feature_slice),
        "expert",
        split_axis=0,
        concat_axis=0,
        tiled=True,
    )
    back_picked = input_back.reshape(slots_total, feature_slice)[target].reshape(
        local_tokens, TOPK, feature_slice
    )
    token_grad = jnp.sum(back_picked.astype(jnp.float32), axis=1).astype(jnp.bfloat16)
    return (mixed_out, token_grad, gate_grad)


def solution(mesh):
    in_specs = (
        P("expert", "dp"),
        P("expert", "dp", None),
        P("expert", "dp", None),
        P("expert", None, "dp"),
        P("expert", None),
        P("expert", None),
        P("expert"),
        P("expert", "dp"),
    )
    out_specs = (P("expert", "dp"), P("expert", "dp"), P("expert", None))
    fits = mesh.shape["dp"] == 4 and mesh.shape["expert"] == 8
    return jax.shard_map(
        grouped if fits else on_device,
        mesh=mesh, in_specs=in_specs, out_specs=out_specs, check_vma=False,
    )
```

```python
import functools
import jax
import jax.numpy as jnp
from jax import lax
from jax.experimental import pallas as pl
from jax.experimental.pallas import tpu as pltpu
from jax.sharding import PartitionSpec as P

EXPERTS = 64
TOPK = 8
CAP = 40
VMEM_BYTES = 50 * 1024 * 1024


def moves(ample):
    count = 400_000_000 if ample else 1000
    return pl.CostEstimate(flops=count, bytes_accessed=count, transcendentals=0)


clip_ratio = 2.0


def dot_nn(a, b):
    return lax.dot_general(a, b, (((1,), (0,)), ((), ())), preferred_element_type=jnp.float32)


def dot_nt(a, b):
    return lax.dot_general(a, b, (((1,), (1,)), ((), ())), preferred_element_type=jnp.float32)


def dot_tn(a, b):
    return lax.dot_general(a, b, (((0,), (0,)), ((), ())), preferred_element_type=jnp.float32)


def one_hot(slots_ref, rows):
    slots = slots_ref[0]
    return slots == lax.broadcasted_iota(jnp.int32, (rows, slots.shape[-1]), 0)


def whole(shape):
    return pl.BlockSpec(shape, lambda g, me: (0,) * len(shape))


def expert_block(shape, halves):
    count = len(halves)
    return pl.BlockSpec(
        (1,) + shape,
        lambda g, me: (2 * ((g // count) ^ me[0]) + (halves[0] + g % count), 0, 0),
    )


def partial_kernel(count, me, same, other, slots, w_gate, w_up, w_down, after,
                   own, part_x, part_y, across_a, across_b):
    step = pl.program_id(0)
    part, half = step // count, step % count
    tokens, width = same.shape
    rows = own.shape[1]
    hidden = w_gate.shape[2]
    cut = across_a.shape[2]
    pick = jnp.where(one_hot(slots, rows), 1.0, 0.0).astype(jnp.bfloat16)
    taken = dot_nn(pick[:, :tokens], same[...]) + dot_nn(pick[:, tokens:], other[...])
    taken = taken.astype(jnp.bfloat16)
    features = width // 2
    gate = dot_nn(taken[:, :features], w_gate[0]).astype(jnp.bfloat16)
    up = dot_nn(taken[:, :features], w_up[0]).astype(jnp.bfloat16)
    back = dot_nt(taken[:, features:], w_down[0]).astype(jnp.bfloat16)
    for v, ref in enumerate((own, part_x, part_y)):
        @pl.when(part == v)
        def _():
            ref[half, :, pl.ds(0, hidden)] = gate
            ref[half, :, pl.ds(hidden, hidden)] = up
            ref[half, :, pl.ds(2 * hidden, hidden)] = back

    @pl.when(part == 3)
    def _():
        across_a[half, :, pl.ds(0, hidden)] = gate
        across_a[half, :, pl.ds(hidden, cut - hidden)] = up[:, : cut - hidden]
        across_b[half, :, pl.ds(0, cut - hidden)] = up[:, cut - hidden :]
        across_b[half, :, pl.ds(cut - hidden, hidden)] = back


def partial_sums(me, same, other, slots, w_gate, w_up, w_down, after, halves, ample):
    count = len(halves)
    features, hidden = w_gate.shape[1:]
    rows, cols = 2 * CAP, 3 * hidden
    full = jax.ShapeDtypeStruct((count, rows, cols), jnp.bfloat16)
    cut = jax.ShapeDtypeStruct((count, rows, cols // 2), jnp.bfloat16)
    outs = (full, full, full, cut, cut)
    steps = 4 * count
    return pl.pallas_call(
        functools.partial(partial_kernel, count),
        grid_spec=pltpu.PrefetchScalarGridSpec(
            num_scalar_prefetch=1,
            grid=(steps,),
            in_specs=[
                whole(same.shape),
                whole(other.shape),
                expert_block(slots.shape[1:], halves),
                expert_block((features, hidden), halves),
                expert_block((features, hidden), halves),
                expert_block((hidden, features), halves),
                pl.BlockSpec(memory_space=pl.ANY),
            ],
            out_specs=[whole(o.shape) for o in outs],
        ),
        out_shape=outs,
        compiler_params=pltpu.CompilerParams(vmem_limit_bytes=VMEM_BYTES),
        cost_estimate=moves(ample),
    )(me, same, other, slots, w_gate, w_up, w_down, after)


def middle_kernel(me, own, from_x, from_y, slots, share, *rest):
    out = rest[-1]
    count, rows, cols = own.shape
    hidden = cols // 3
    half = hidden // 2
    extra = 2 * EXPERTS
    for h in range(count):
        def total(lo):
            cut = pl.ds(lo, half)
            return (
                own[h, :, cut].astype(jnp.float32)
                + from_x[h, :, cut].astype(jnp.float32)
                + from_y[h, :, cut].astype(jnp.float32)
            )
        hot = one_hot(slots.at[pl.ds(h, 1)], rows)
        fraction = jnp.sum(jnp.where(hot, share[h], 0.0), axis=1, keepdims=True)
        grads = jnp.zeros((rows, 1), jnp.float32)
        for side in range(2):
            lo = side * half
            gate, up, back = total(lo), total(hidden + lo), total(2 * hidden + lo)
            sig = 1.0 / (1.0 + jnp.exp(-gate))
            silu = gate * sig
            act = silu * up
            grads = grads + jnp.sum(act * back, axis=1, keepdims=True)
            hidden_grad = back * fraction
            act_out = (act * fraction).astype(jnp.bfloat16)
            gate_out = (hidden_grad * up * sig * (1.0 + gate * (1.0 - sig))).astype(jnp.bfloat16)
            up_out = (hidden_grad * silu).astype(jnp.bfloat16)
            out[h, :, pl.ds(lo, half)] = act_out
            out[h, :, pl.ds(hidden + side * (half + extra), half)] = gate_out
            out[h, :, pl.ds(2 * hidden + extra + lo, half)] = up_out
        lane = lax.broadcasted_iota(jnp.int32, (rows, extra), 1)
        high = grads.astype(jnp.bfloat16).astype(jnp.float32)
        spread = jnp.where(lane == me[0] + h, high, 0.0)
        spread = jnp.where(lane == me[0] + h + EXPERTS, grads - high, spread)
        out[h, :, pl.ds(cols // 2, extra)] = spread.astype(jnp.bfloat16)


def at_once(shape):
    return pl.BlockSpec(shape, lambda g: (0,) * len(shape))


def middle(first, own, from_x, from_y, slots, share, after, ample):
    count, rows, cols = own.shape
    out = jax.ShapeDtypeStruct((count, rows, cols + 2 * EXPERTS), jnp.bfloat16)
    return pl.pallas_call(
        middle_kernel,
        grid=(1,),
        out_shape=out,
        in_specs=[pl.BlockSpec(memory_space=pltpu.SMEM)]
        + [at_once(a.shape) for a in (own, from_x, from_y, slots, share)]
        + [pl.BlockSpec(memory_space=pl.ANY)] * len(after),
        out_specs=at_once(out.shape),
        compiler_params=pltpu.CompilerParams(vmem_limit_bytes=VMEM_BYTES),
        cost_estimate=moves(ample),
    )(first, own, from_x, from_y, slots, share, *after)


def between_kernel(waits, adds, relays, passes, *refs):
    count = 4 * adds + 2 * relays + passes
    ins, outs = list(refs[:count]), list(refs[count + waits :])
    if adds:
        part_x, part_y, given_a, given_b = ins[:4]
        to_x, to_y = outs[:2]
        cut = given_a.shape[2]
        low, high = pl.ds(0, cut), pl.ds(cut, cut)
        to_x[:, :, low] = part_x[:, :, low]
        to_x[:, :, high] = (
            part_x[:, :, high].astype(jnp.float32) + given_b[...].astype(jnp.float32)
        ).astype(jnp.bfloat16)
        to_y[:, :, low] = (
            part_y[:, :, low].astype(jnp.float32) + given_a[...].astype(jnp.float32)
        ).astype(jnp.bfloat16)
        to_y[:, :, high] = part_y[:, :, high]
        ins, outs = ins[4:], outs[2:]
    if relays:
        rows_x, rows_y = ins[:2]
        out_a, out_b = outs[:2]
        cut = out_a.shape[2]
        out_a[...] = rows_y[:, :, pl.ds(0, cut)]
        out_b[...] = rows_x[:, :, pl.ds(cut, out_b.shape[2])]
        ins, outs = ins[2:], outs[2:]
    if passes:
        outs[0][...] = ins[0][...]


def between(add, relay, block, after, ample):
    ins, outs = [], []
    if add is not None:
        ins += add
        outs += [add[0].shape, add[1].shape]
    if relay is not None:
        ins += relay
        count, rows, width = relay[0].shape
        cols = (width - 2 * EXPERTS) // 2
        outs += [(count, rows, cols + 2 * EXPERTS), (count, rows, cols)]
    if block is not None:
        ins += [block]
        outs += [block.shape]
    given = [int(a is not None) for a in (add, relay, block)]
    return pl.pallas_call(
        functools.partial(between_kernel, len(after), *given),
        grid=(1,),
        out_shape=[jax.ShapeDtypeStruct(o, jnp.bfloat16) for o in outs],
        in_specs=[at_once(i.shape) for i in ins]
        + [pl.BlockSpec(memory_space=pl.ANY)] * len(after),
        out_specs=[at_once(o) for o in outs],
        compiler_params=pltpu.CompilerParams(vmem_limit_bytes=VMEM_BYTES),
        cost_estimate=moves(ample),
    )(*ins, *after)


def add_up_kernel(count, *refs):
    ins, outs = refs[:count], refs[count + 1 :]
    for n, out in enumerate(outs):
        cut = pl.ds(n * out.shape[0], out.shape[0])
        total = ins[0][cut, :].astype(jnp.float32)
        for ref in ins[1:]:
            total = total + ref[cut, :].astype(jnp.float32)
        out[...] = total.astype(jnp.bfloat16)


def add_up(blocks, splits, after):
    rows, width = blocks[0].shape
    out = jax.ShapeDtypeStruct((rows // splits, width), jnp.bfloat16)
    return pl.pallas_call(
        functools.partial(add_up_kernel, len(blocks)),
        grid=(1,),
        out_shape=[out] * splits,
        in_specs=[at_once((rows, width))] * len(blocks) + [pl.BlockSpec(memory_space=pl.ANY)],
        out_specs=[at_once(out.shape)] * splits,
        compiler_params=pltpu.CompilerParams(vmem_limit_bytes=VMEM_BYTES),
        cost_estimate=moves(True),
    )(*blocks, after)


def combine_kernel(count, waits, me, *refs):
    across_a, across_b = refs[3:5]
    slots, w_gate, w_up, w_down = refs[5:9]
    same, other, rows_in, hots, outs = refs[9 + waits :]
    step = pl.program_id(0)
    part, half = step // count, step % count
    rows, cols = rows_in.shape[0], across_b.shape[2]
    extra = pl.ds(cols, 2 * EXPERTS)
    hidden = w_gate.shape[2]
    features = w_gate.shape[1]
    at = pl.ds(pl.multiple_of(step * rows, 16), rows)
    for v in range(4):
        @pl.when(part == v)
        def _():
            left = refs[v] if v < 3 else across_a
            rows_in[:, pl.ds(0, cols)] = left[half, :, pl.ds(0, cols)]
            outs[at, pl.ds(2 * features, 2 * EXPERTS)] = left[half, :, extra]
            if v < 3:
                rows_in[:, pl.ds(cols, cols)] = left[half, :, pl.ds(cols + 2 * EXPERTS, cols)]
            else:
                rows_in[:, pl.ds(cols, cols)] = across_b[half]
    outs[at, pl.ds(0, features)] = dot_nn(rows_in[:, pl.ds(0, hidden)], w_down[0]).astype(jnp.bfloat16)
    outs[at, pl.ds(features, features)] = (
        dot_nt(rows_in[:, pl.ds(hidden, hidden)], w_gate[0])
        + dot_nt(rows_in[:, pl.ds(2 * hidden, hidden)], w_up[0])
    ).astype(jnp.bfloat16)
    hots[at, :] = jnp.where(one_hot(slots, rows), 1.0, 0.0).astype(jnp.bfloat16)

    @pl.when(step == pl.num_programs(0) - 1)
    def _():
        tokens, width = same.shape
        for ref, lo in ((same, 0), (other, tokens)):
            ref[...] = dot_tn(hots[:, pl.ds(lo, tokens)], outs[...]).astype(jnp.bfloat16)


def combine(me, given, slots, w_gate, w_up, w_down, after, halves, ample=True):
    count = len(halves)
    features, hidden = w_gate.shape[1:]
    rows = 2 * CAP
    tokens = slots.shape[2] // 2
    steps = 4 * count
    width = 2 * features + 2 * EXPERTS
    out = jax.ShapeDtypeStruct((tokens, width), jnp.bfloat16)
    return pl.pallas_call(
        functools.partial(combine_kernel, count, len(after)),
        grid_spec=pltpu.PrefetchScalarGridSpec(
            num_scalar_prefetch=1,
            grid=(steps,),
            in_specs=[whole(a.shape) for a in given]
            + [
                expert_block(slots.shape[1:], halves),
                expert_block((features, hidden), halves),
                expert_block((features, hidden), halves),
                expert_block((hidden, features), halves),
                *[pl.BlockSpec(memory_space=pl.ANY)] * len(after),
            ],
            out_specs=[whole(out.shape)] * 2,
            scratch_shapes=[
                pltpu.VMEM((rows, 3 * hidden), jnp.bfloat16),
                pltpu.VMEM((steps * rows, 2 * tokens), jnp.bfloat16),
                pltpu.VMEM((steps * rows, width), jnp.bfloat16),
            ],
        ),
        out_shape=(out, out),
        compiler_params=pltpu.CompilerParams(vmem_limit_bytes=VMEM_BYTES),
        cost_estimate=moves(ample),
    )(me, *given, slots, w_gate, w_up, w_down, *after)


def swap(value, axis, bits):
    count = lax.axis_size(axis)
    return lax.ppermute(value, axis, [(n, n ^ bits) for n in range(count)])


def grouped(tokens, gate_weight, up_weight, down_weight, routes, gate_levels, log_ratio, cotangent):
    block, features = tokens.shape
    per_device = gate_weight.shape[0]
    peers = lax.axis_size("expert")
    chips = peers // 2
    mine = lax.axis_index("expert")
    member = lax.axis_index("dp")
    me = member.astype(jnp.int32).reshape(1)

    ratio_weight = jnp.minimum(jnp.exp(log_ratio), clip_ratio)
    weighted = (ratio_weight[:, None] * cotangent.astype(jnp.float32)).astype(jnp.bfloat16)
    payload = jnp.concatenate([tokens, weighted], axis=1)
    arriving = swap(payload, "expert", 6)
    sames = {0: payload, 1: swap(payload, "expert", 2)}
    others = {0: swap(payload, "expert", 1)}

    local = mine * per_device + jnp.arange(per_device, dtype=jnp.int32)
    tri = (jnp.arange(block)[:, None] < jnp.arange(block)[None, :]).astype(jnp.bfloat16)

    def placed(picks):
        levels = picks[:, 1].astype(jnp.float32)
        fractions = levels / jnp.sum(levels, axis=1, keepdims=True)
        named = picks[:, 0][None] == local[:, None, None, None]
        share = jnp.sum(jnp.where(named, fractions[None], 0.0), axis=2)
        chosen = jnp.any(named, axis=2)
        place = jnp.einsum(
            "jst,tu->jsu", chosen.astype(jnp.bfloat16), tri, preferred_element_type=jnp.float32
        ).astype(jnp.int32)
        place = place + (jnp.arange(picks.shape[0], dtype=jnp.int32) % 2 * CAP)[None, :, None]
        slots = jnp.where(chosen, place, -1)
        pairs = (per_device, picks.shape[0] // 2, 1, 2 * block)
        return slots.reshape(pairs), share.reshape(pairs)

    picks = jnp.stack([routes.T, gate_levels.T])
    near = jnp.stack([picks, swap(picks, "expert", 1)])
    away = jnp.stack([swap(picks, "expert", 2 * o) for o in range(1, chips)])
    far = jnp.stack([away, swap(away, "expert", 1)], axis=1).reshape(-1, *picks.shape)
    near_slots, near_share = placed(near)
    far_slots, far_share = placed(far)

    weights = (gate_weight, up_weight, down_weight)
    chunks = [(0, (0,)), (3, (0, 1)), (2, (0, 1)), (1, (0, 1)), (0, (1,))]
    sums, adds, sent, got, relayed, blocks = {}, {}, {}, {}, {}, {}
    after = near_slots

    def slots_of(k):
        o = chunks[k][0]
        return far_slots[:, o - 1] if o else near_slots[:, 0]

    def share_of(k):
        o = chunks[k][0]
        return far_share[:, o - 1] if o else near_share[:, 0]

    def start_rows(k, after):
        o, halves = chunks[k]
        own, part_x, part_y, across_a, across_b = partial_sums(
            me, sames[o], others[o], slots_of(k), *weights, after, halves, k > 0
        )
        sums[k] = own
        adds[k] = [part_x, part_y, swap(across_a, "dp", 1), swap(across_b, "dp", 2)]
        return own

    def move(k, r, *after, block=None):
        outs = between(adds.get(k), got.get(r), block, after, k != 0 and r != 0)
        if k in adds:
            sums[k] = sums[k], swap(outs[0], "dp", 1), swap(outs[1], "dp", 2)
        if r in got:
            at = 2 if k in adds else 0
            relayed[r] = swap(outs[at], "dp", 1), swap(outs[at + 1], "dp", 2)
        if block is not None:
            return outs[0], outs[-1], swap(outs[-1], "expert", 1)
        return outs[0]

    def turn_rows(k, *after):
        halves = chunks[k][1]
        first = 2 * member + halves[0]
        own_slot = lax.dynamic_slice_in_dim(slots_of(k), first, len(halves), 0)
        own_share = lax.dynamic_slice_in_dim(share_of(k), first, len(halves), 0)
        expert = (mine * per_device + first).astype(jnp.int32).reshape(1)
        sent[k] = middle(expert, *sums[k], own_slot, own_share, after, k > 0)
        got[k] = [swap(sent[k], "dp", 1), swap(sent[k], "dp", 2)]
        return sent[k]

    def finish_rows(k, *after):
        o, halves = chunks[k]
        given = (sent[k], *got[k], *relayed[k])
        same, other = combine(me, given, slots_of(k), *weights, after, halves)
        blocks[k] = [same, other]
        return same

    after = start_rows(0, after)
    after = move(0, None, after)
    after = turn_rows(0, after)
    after, sames[3], others[3] = move(None, 0, after, block=arriving)
    sames[2] = swap(sames[3], "expert", 2)
    after = start_rows(1, after)
    after, sames[2], others[2] = move(1, None, after, *relayed[0], block=sames[2])
    after = start_rows(2, after)
    after = turn_rows(1, after)
    after = finish_rows(0, after)
    after, sames[1], others[1] = move(2, 1, after, block=sames[1])
    after = start_rows(3, after)
    after = turn_rows(2, after, *relayed[1])
    after = finish_rows(1, after)
    after, _, other = move(3, 2, after, block=blocks[1][1])
    after = start_rows(4, after)
    (after,) = add_up([blocks[1][0], other], 1, after)
    hop = swap(after, "expert", 2)
    after = turn_rows(3, after, *relayed[2], *adds[4][2:])
    after = finish_rows(2, after)
    after, _, other = move(4, 3, after, hop, block=blocks[2][1])
    after, second = add_up([blocks[2][0], other, hop], 2, after)
    far_low, far_high = swap(after, "expert", 4), swap(second, "expert", 4)
    after = turn_rows(4, second, *relayed[3])
    after = finish_rows(3, after)
    after, _, other = move(None, 4, after, far_low, block=blocks[3][1])
    (after,) = add_up([blocks[3][0], other], 1, after)
    near_back = swap(after, "expert", 2)
    after = finish_rows(4, after)
    for k in (0, 4):
        blocks[k][1] = swap(blocks[k][1], "expert", 1)
    far_back = jnp.concatenate([far_low, far_high], axis=0)
    total = sum(t.astype(jnp.float32) for t in (*blocks[0], *blocks[4], near_back, far_back))
    grads = total[:, 2 * features : 2 * features + EXPERTS] + total[:, 2 * features + EXPERTS :]
    hit = routes[:, :, None] == jnp.arange(EXPERTS, dtype=jnp.int32)
    gate_grad = jnp.sum(jnp.where(hit, grads[:, None, :], 0.0), axis=2)
    total = total[:, : 2 * features].astype(jnp.bfloat16)
    return total[:, :features], total[:, features:], gate_grad


def on_device(
    tokens, gate_weight, up_weight, down_weight, routes, gate_levels, log_ratio, cotangent
):
    local_tokens = tokens.shape[0]
    feature_slice = tokens.shape[1]
    hidden = gate_weight.shape[2]
    per_device = gate_weight.shape[0]
    peer_count = lax.axis_size("expert")
    slots_total = EXPERTS * CAP
    pick_ids = routes.reshape(-1)
    onehot_table = (pick_ids[:, None] == jnp.arange(EXPERTS, dtype=jnp.int32)[None, :]).astype(
        jnp.int32
    )
    earlier = jnp.cumsum(onehot_table, axis=0) - onehot_table
    position = jnp.sum(earlier * onehot_table, axis=1)
    target = pick_ids * CAP + position

    def pack_rows(values):
        packed = jnp.zeros((slots_total, feature_slice), jnp.bfloat16).at[target].set(values)
        return packed.reshape(peer_count, per_device * CAP, feature_slice)

    received = lax.all_to_all(
        pack_rows(jnp.repeat(tokens, TOPK, axis=0)),
        "expert",
        split_axis=0,
        concat_axis=0,
        tiled=True,
    )
    arrived = received.reshape(peer_count, per_device, CAP, feature_slice)
    gate_part = jnp.einsum(
        "sjcd,jdf->sjcf", arrived, gate_weight, preferred_element_type=jnp.float32
    ).reshape(-1, hidden)
    up_part = jnp.einsum(
        "sjcd,jdf->sjcf", arrived, up_weight, preferred_element_type=jnp.float32
    ).reshape(-1, hidden)
    gate_share, up_share = (
        lax.psum_scatter(gate_part, "dp", scatter_dimension=0, tiled=True),
        lax.psum_scatter(up_part, "dp", scatter_dimension=0, tiled=True),
    )
    activated = lax.all_gather(
        (jax.nn.silu(gate_share) * up_share).astype(jnp.bfloat16), "dp", axis=0, tiled=True
    )
    expert_out = jnp.einsum(
        "sjcf,jfd->sjcd",
        activated.reshape(peer_count, per_device, CAP, hidden),
        down_weight,
        preferred_element_type=jnp.float32,
    ).astype(jnp.bfloat16)
    returned = lax.all_to_all(
        expert_out.reshape(peer_count, per_device * CAP, feature_slice),
        "expert",
        split_axis=0,
        concat_axis=0,
        tiled=True,
    )
    picked = (
        returned.reshape(slots_total, feature_slice)[target]
        .reshape(local_tokens, TOPK, feature_slice)
        .astype(jnp.float32)
    )
    levels = gate_levels.astype(jnp.float32)
    fractions = levels / jnp.sum(levels, axis=1, keepdims=True)
    mixed_out = jnp.sum(fractions[:, :, None] * picked, axis=1).astype(jnp.bfloat16)
    ratio_weight = jnp.minimum(jnp.exp(log_ratio), clip_ratio)
    weighted = (ratio_weight[:, None] * cotangent.astype(jnp.float32)).astype(jnp.bfloat16)
    weighted_wide = weighted.astype(jnp.float32)[:, None, :]
    gate_grad = lax.psum(jnp.sum(weighted_wide * picked, axis=2), "dp")
    pick_grad = (
        (fractions[:, :, None] * weighted_wide).astype(jnp.bfloat16).reshape(-1, feature_slice)
    )
    back_rows = lax.all_to_all(
        pack_rows(pick_grad), "expert", split_axis=0, concat_axis=0, tiled=True
    )
    back_rows = back_rows.reshape(peer_count, per_device, CAP, feature_slice)
    hidden_part = jnp.einsum(
        "sjcd,jfd->sjcf", back_rows, down_weight, preferred_element_type=jnp.float32
    ).reshape(-1, hidden)
    hidden_grad = lax.psum_scatter(hidden_part, "dp", scatter_dimension=0, tiled=True)
    sigmoid_gate = jax.nn.sigmoid(gate_share)
    gate_back = (
        hidden_grad * up_share * sigmoid_gate * (1.0 + gate_share * (1.0 - sigmoid_gate))
    ).astype(jnp.bfloat16)
    up_back = (hidden_grad * gate_share * sigmoid_gate).astype(jnp.bfloat16)
    gate_rows, up_rows = (
        lax.all_gather(gate_back, "dp", axis=0, tiled=True),
        lax.all_gather(up_back, "dp", axis=0, tiled=True),
    )
    gate_rows = gate_rows.reshape(peer_count, per_device, CAP, hidden)
    up_rows = up_rows.reshape(peer_count, per_device, CAP, hidden)
    input_part = jnp.einsum(
        "sjcf,jdf->sjcd", gate_rows, gate_weight, preferred_element_type=jnp.float32
    )
    input_part = (
        input_part
        + jnp.einsum("sjcf,jdf->sjcd", up_rows, up_weight, preferred_element_type=jnp.float32)
    ).astype(jnp.bfloat16)
    input_back = lax.all_to_all(
        input_part.reshape(peer_count, per_device * CAP, feature_slice),
        "expert",
        split_axis=0,
        concat_axis=0,
        tiled=True,
    )
    back_picked = input_back.reshape(slots_total, feature_slice)[target].reshape(
        local_tokens, TOPK, feature_slice
    )
    token_grad = jnp.sum(back_picked.astype(jnp.float32), axis=1).astype(jnp.bfloat16)
    return (mixed_out, token_grad, gate_grad)


def solution(mesh):
    in_specs = (
        P("expert", "dp"),
        P("expert", "dp", None),
        P("expert", "dp", None),
        P("expert", None, "dp"),
        P("expert", None),
        P("expert", None),
        P("expert"),
        P("expert", "dp"),
    )
    out_specs = (P("expert", "dp"), P("expert", "dp"), P("expert", None))
    fits = mesh.shape["dp"] == 4 and mesh.shape["expert"] == 8
    return jax.shard_map(
        grouped if fits else on_device,
        mesh=mesh, in_specs=in_specs, out_specs=out_specs, check_vma=False,
    )
```

```python
import functools
import jax
import jax.numpy as jnp
from jax import lax
from jax.experimental import pallas as pl
from jax.experimental.pallas import tpu as pltpu
from jax.sharding import PartitionSpec as P

EXPERTS = 64
TOPK = 8
CAP = 40
VMEM_BYTES = 50 * 1024 * 1024


def moves(ample):
    count = 400_000_000 if ample else 1000
    return pl.CostEstimate(flops=count, bytes_accessed=count, transcendentals=0)


clip_ratio = 2.0


def dot_nn(a, b):
    return lax.dot_general(a, b, (((1,), (0,)), ((), ())), preferred_element_type=jnp.float32)


def dot_nt(a, b):
    return lax.dot_general(a, b, (((1,), (1,)), ((), ())), preferred_element_type=jnp.float32)


def dot_tn(a, b):
    return lax.dot_general(a, b, (((0,), (0,)), ((), ())), preferred_element_type=jnp.float32)


def one_hot(slots_ref, rows):
    slots = slots_ref[0]
    return slots == lax.broadcasted_iota(jnp.int32, (rows, slots.shape[-1]), 0)


def whole(shape):
    return pl.BlockSpec(shape, lambda g, me: (0,) * len(shape))


def expert_block(shape, halves):
    count = len(halves)
    return pl.BlockSpec(
        (1,) + shape,
        lambda g, me: (2 * ((g // count) ^ me[0]) + (halves[0] + g % count), 0, 0),
    )


def partial_kernel(count, me, same, other, slots, w_gate, w_up, w_down, *rest):
    own, part_x, part_y, across_a, across_b = rest[-5:]
    step = pl.program_id(0)
    part, half = step // count, step % count
    tokens, width = same.shape
    rows = own.shape[1]
    hidden = w_gate.shape[2]
    cut = across_a.shape[2]
    pick = jnp.where(one_hot(slots, rows), 1.0, 0.0).astype(jnp.bfloat16)
    taken = dot_nn(pick[:, :tokens], same[...]) + dot_nn(pick[:, tokens:], other[...])
    taken = taken.astype(jnp.bfloat16)
    features = width // 2
    gate = dot_nn(taken[:, :features], w_gate[0]).astype(jnp.bfloat16)
    up = dot_nn(taken[:, :features], w_up[0]).astype(jnp.bfloat16)
    back = dot_nt(taken[:, features:], w_down[0]).astype(jnp.bfloat16)
    for v, ref in enumerate((own, part_x, part_y)):
        @pl.when(part == v)
        def _():
            ref[half, :, pl.ds(0, hidden)] = gate
            ref[half, :, pl.ds(hidden, hidden)] = up
            ref[half, :, pl.ds(2 * hidden, hidden)] = back

    @pl.when(part == 3)
    def _():
        across_a[half, :, pl.ds(0, hidden)] = gate
        across_a[half, :, pl.ds(hidden, cut - hidden)] = up[:, : cut - hidden]
        across_b[half, :, pl.ds(0, cut - hidden)] = up[:, cut - hidden :]
        across_b[half, :, pl.ds(cut - hidden, hidden)] = back


def partial_sums(me, same, other, slots, w_gate, w_up, w_down, after, halves, ample):
    count = len(halves)
    features, hidden = w_gate.shape[1:]
    rows, cols = 2 * CAP, 3 * hidden
    full = jax.ShapeDtypeStruct((count, rows, cols), jnp.bfloat16)
    cut = jax.ShapeDtypeStruct((count, rows, cols // 2), jnp.bfloat16)
    outs = (full, full, full, cut, cut)
    steps = 4 * count
    return pl.pallas_call(
        functools.partial(partial_kernel, count),
        grid_spec=pltpu.PrefetchScalarGridSpec(
            num_scalar_prefetch=1,
            grid=(steps,),
            in_specs=[
                whole(same.shape),
                whole(other.shape),
                expert_block(slots.shape[1:], halves),
                expert_block((features, hidden), halves),
                expert_block((features, hidden), halves),
                expert_block((hidden, features), halves),
                *[pl.BlockSpec(memory_space=pl.ANY)] * len(after),
            ],
            out_specs=[whole(o.shape) for o in outs],
        ),
        out_shape=outs,
        compiler_params=pltpu.CompilerParams(vmem_limit_bytes=VMEM_BYTES),
        cost_estimate=moves(ample),
    )(me, same, other, slots, w_gate, w_up, w_down, *after)


def middle_kernel(me, own, from_x, from_y, slots, share, *rest):
    out = rest[-1]
    count, rows, cols = own.shape
    hidden = cols // 3
    half = hidden // 2
    extra = 2 * EXPERTS
    for h in range(count):
        def total(lo):
            cut = pl.ds(lo, half)
            return (
                own[h, :, cut].astype(jnp.float32)
                + from_x[h, :, cut].astype(jnp.float32)
                + from_y[h, :, cut].astype(jnp.float32)
            )
        hot = one_hot(slots.at[pl.ds(h, 1)], rows)
        fraction = jnp.sum(jnp.where(hot, share[h], 0.0), axis=1, keepdims=True)
        grads = jnp.zeros((rows, 1), jnp.float32)
        for side in range(2):
            lo = side * half
            gate, up, back = total(lo), total(hidden + lo), total(2 * hidden + lo)
            sig = 1.0 / (1.0 + jnp.exp(-gate))
            silu = gate * sig
            act = silu * up
            grads = grads + jnp.sum(act * back, axis=1, keepdims=True)
            hidden_grad = back * fraction
            act_out = (act * fraction).astype(jnp.bfloat16)
            gate_out = (hidden_grad * up * sig * (1.0 + gate * (1.0 - sig))).astype(jnp.bfloat16)
            up_out = (hidden_grad * silu).astype(jnp.bfloat16)
            out[h, :, pl.ds(lo, half)] = act_out
            out[h, :, pl.ds(hidden + side * (half + extra), half)] = gate_out
            out[h, :, pl.ds(2 * hidden + extra + lo, half)] = up_out
        lane = lax.broadcasted_iota(jnp.int32, (rows, extra), 1)
        high = grads.astype(jnp.bfloat16).astype(jnp.float32)
        spread = jnp.where(lane == me[0] + h, high, 0.0)
        spread = jnp.where(lane == me[0] + h + EXPERTS, grads - high, spread)
        out[h, :, pl.ds(cols // 2, extra)] = spread.astype(jnp.bfloat16)


def at_once(shape):
    return pl.BlockSpec(shape, lambda g: (0,) * len(shape))


def middle(first, own, from_x, from_y, slots, share, after, ample):
    count, rows, cols = own.shape
    out = jax.ShapeDtypeStruct((count, rows, cols + 2 * EXPERTS), jnp.bfloat16)
    return pl.pallas_call(
        middle_kernel,
        grid=(1,),
        out_shape=out,
        in_specs=[pl.BlockSpec(memory_space=pltpu.SMEM)]
        + [at_once(a.shape) for a in (own, from_x, from_y, slots, share)]
        + [pl.BlockSpec(memory_space=pl.ANY)] * len(after),
        out_specs=at_once(out.shape),
        compiler_params=pltpu.CompilerParams(vmem_limit_bytes=VMEM_BYTES),
        cost_estimate=moves(ample),
    )(first, own, from_x, from_y, slots, share, *after)


def between_kernel(waits, adds, relays, passes, *refs):
    count = 4 * adds + 2 * relays + passes
    ins, outs = list(refs[:count]), list(refs[count + waits :])
    if adds:
        part_x, part_y, given_a, given_b = ins[:4]
        to_x, to_y = outs[:2]
        cut = given_a.shape[2]
        low, high = pl.ds(0, cut), pl.ds(cut, cut)
        to_x[:, :, low] = part_x[:, :, low]
        to_x[:, :, high] = (
            part_x[:, :, high].astype(jnp.float32) + given_b[...].astype(jnp.float32)
        ).astype(jnp.bfloat16)
        to_y[:, :, low] = (
            part_y[:, :, low].astype(jnp.float32) + given_a[...].astype(jnp.float32)
        ).astype(jnp.bfloat16)
        to_y[:, :, high] = part_y[:, :, high]
        ins, outs = ins[4:], outs[2:]
    if relays:
        rows_x, rows_y = ins[:2]
        out_a, out_b = outs[:2]
        cut = out_a.shape[2]
        out_a[...] = rows_y[:, :, pl.ds(0, cut)]
        out_b[...] = rows_x[:, :, pl.ds(cut, out_b.shape[2])]
        ins, outs = ins[2:], outs[2:]
    if passes:
        outs[0][...] = ins[0][...]


def between(add, relay, block, after, ample):
    ins, outs = [], []
    if add is not None:
        ins += add
        outs += [add[0].shape, add[1].shape]
    if relay is not None:
        ins += relay
        count, rows, width = relay[0].shape
        cols = (width - 2 * EXPERTS) // 2
        outs += [(count, rows, cols + 2 * EXPERTS), (count, rows, cols)]
    if block is not None:
        ins += [block]
        outs += [block.shape]
    given = [int(a is not None) for a in (add, relay, block)]
    return pl.pallas_call(
        functools.partial(between_kernel, len(after), *given),
        grid=(1,),
        out_shape=[jax.ShapeDtypeStruct(o, jnp.bfloat16) for o in outs],
        in_specs=[at_once(i.shape) for i in ins]
        + [pl.BlockSpec(memory_space=pl.ANY)] * len(after),
        out_specs=[at_once(o) for o in outs],
        compiler_params=pltpu.CompilerParams(vmem_limit_bytes=VMEM_BYTES),
        cost_estimate=moves(ample),
    )(*ins, *after)


def add_up_kernel(count, waits, *refs):
    ins, outs = refs[:count], refs[count + waits :]
    for n, out in enumerate(outs):
        cut = pl.ds(n * out.shape[0], out.shape[0])
        total = ins[0][cut, :].astype(jnp.float32)
        for ref in ins[1:]:
            total = total + ref[cut, :].astype(jnp.float32)
        out[...] = total.astype(jnp.bfloat16)


def add_up(blocks, splits, *after):
    rows, width = blocks[0].shape
    out = jax.ShapeDtypeStruct((rows // splits, width), jnp.bfloat16)
    return pl.pallas_call(
        functools.partial(add_up_kernel, len(blocks), len(after)),
        grid=(1,),
        out_shape=[out] * splits,
        in_specs=[at_once((rows, width))] * len(blocks)
        + [pl.BlockSpec(memory_space=pl.ANY)] * len(after),
        out_specs=[at_once(out.shape)] * splits,
        compiler_params=pltpu.CompilerParams(vmem_limit_bytes=VMEM_BYTES),
        cost_estimate=moves(True),
    )(*blocks, *after)


def combine_kernel(count, waits, me, *refs):
    across_a, across_b = refs[3:5]
    slots, w_gate, w_up, w_down = refs[5:9]
    same, other, rows_in, hots, outs = refs[9 + waits :]
    step = pl.program_id(0)
    part, half = step // count, step % count
    rows, cols = rows_in.shape[0], across_b.shape[2]
    extra = pl.ds(cols, 2 * EXPERTS)
    hidden = w_gate.shape[2]
    features = w_gate.shape[1]
    at = pl.ds(pl.multiple_of(step * rows, 16), rows)
    for v in range(4):
        @pl.when(part == v)
        def _():
            left = refs[v] if v < 3 else across_a
            rows_in[:, pl.ds(0, cols)] = left[half, :, pl.ds(0, cols)]
            outs[at, pl.ds(2 * features, 2 * EXPERTS)] = left[half, :, extra]
            if v < 3:
                rows_in[:, pl.ds(cols, cols)] = left[half, :, pl.ds(cols + 2 * EXPERTS, cols)]
            else:
                rows_in[:, pl.ds(cols, cols)] = across_b[half]
    outs[at, pl.ds(0, features)] = dot_nn(rows_in[:, pl.ds(0, hidden)], w_down[0]).astype(jnp.bfloat16)
    outs[at, pl.ds(features, features)] = (
        dot_nt(rows_in[:, pl.ds(hidden, hidden)], w_gate[0])
        + dot_nt(rows_in[:, pl.ds(2 * hidden, hidden)], w_up[0])
    ).astype(jnp.bfloat16)
    hots[at, :] = jnp.where(one_hot(slots, rows), 1.0, 0.0).astype(jnp.bfloat16)

    @pl.when(step == pl.num_programs(0) - 1)
    def _():
        tokens, width = same.shape
        for ref, lo in ((same, 0), (other, tokens)):
            ref[...] = dot_tn(hots[:, pl.ds(lo, tokens)], outs[...]).astype(jnp.bfloat16)


def combine(me, given, slots, w_gate, w_up, w_down, after, halves, ample=True):
    count = len(halves)
    features, hidden = w_gate.shape[1:]
    rows = 2 * CAP
    tokens = slots.shape[2] // 2
    steps = 4 * count
    width = 2 * features + 2 * EXPERTS
    out = jax.ShapeDtypeStruct((tokens, width), jnp.bfloat16)
    return pl.pallas_call(
        functools.partial(combine_kernel, count, len(after)),
        grid_spec=pltpu.PrefetchScalarGridSpec(
            num_scalar_prefetch=1,
            grid=(steps,),
            in_specs=[whole(a.shape) for a in given]
            + [
                expert_block(slots.shape[1:], halves),
                expert_block((features, hidden), halves),
                expert_block((features, hidden), halves),
                expert_block((hidden, features), halves),
                *[pl.BlockSpec(memory_space=pl.ANY)] * len(after),
            ],
            out_specs=[whole(out.shape)] * 2,
            scratch_shapes=[
                pltpu.VMEM((rows, 3 * hidden), jnp.bfloat16),
                pltpu.VMEM((steps * rows, 2 * tokens), jnp.bfloat16),
                pltpu.VMEM((steps * rows, width), jnp.bfloat16),
            ],
        ),
        out_shape=(out, out),
        compiler_params=pltpu.CompilerParams(vmem_limit_bytes=VMEM_BYTES),
        cost_estimate=moves(ample),
    )(me, *given, slots, w_gate, w_up, w_down, *after)


def swap(value, axis, bits):
    count = lax.axis_size(axis)
    return lax.ppermute(value, axis, [(n, n ^ bits) for n in range(count)])


def grouped(tokens, gate_weight, up_weight, down_weight, routes, gate_levels, log_ratio, cotangent):
    block, features = tokens.shape
    per_device = gate_weight.shape[0]
    peers = lax.axis_size("expert")
    chips = peers // 2
    mine = lax.axis_index("expert")
    member = lax.axis_index("dp")
    me = member.astype(jnp.int32).reshape(1)

    ratio_weight = jnp.minimum(jnp.exp(log_ratio), clip_ratio)
    weighted = (ratio_weight[:, None] * cotangent.astype(jnp.float32)).astype(jnp.bfloat16)
    payload = jnp.concatenate([tokens, weighted], axis=1)
    arriving = swap(payload, "expert", 6)
    sames = {0: payload, 1: swap(payload, "expert", 2)}
    others = {0: swap(payload, "expert", 1)}

    local = mine * per_device + jnp.arange(per_device, dtype=jnp.int32)
    tri = (jnp.arange(block)[:, None] < jnp.arange(block)[None, :]).astype(jnp.bfloat16)

    def placed(picks):
        levels = picks[:, 1].astype(jnp.float32)
        fractions = levels / jnp.sum(levels, axis=1, keepdims=True)
        named = picks[:, 0][None] == local[:, None, None, None]
        share = jnp.sum(jnp.where(named, fractions[None], 0.0), axis=2)
        chosen = jnp.any(named, axis=2)
        place = jnp.einsum(
            "jst,tu->jsu", chosen.astype(jnp.bfloat16), tri, preferred_element_type=jnp.float32
        ).astype(jnp.int32)
        place = place + (jnp.arange(picks.shape[0], dtype=jnp.int32) % 2 * CAP)[None, :, None]
        slots = jnp.where(chosen, place, -1)
        pairs = (per_device, picks.shape[0] // 2, 1, 2 * block)
        return slots.reshape(pairs), share.reshape(pairs)

    picks = jnp.stack([routes.T, gate_levels.T])
    near = jnp.stack([picks, swap(picks, "expert", 1)])
    away = jnp.stack([swap(picks, "expert", 2 * o) for o in range(1, chips)])
    far = jnp.stack([away, swap(away, "expert", 1)], axis=1).reshape(-1, *picks.shape)
    near_slots, near_share = placed(near)
    far_slots, far_share = placed(far)

    weights = (gate_weight, up_weight, down_weight)
    chunks = [(0, (0,)), (3, (0, 1)), (2, (0, 1)), (1, (0, 1)), (0, (1,))]
    sums, adds, sent, got, relayed, blocks = {}, {}, {}, {}, {}, {}
    after = near_slots

    def slots_of(k):
        o = chunks[k][0]
        return far_slots[:, o - 1] if o else near_slots[:, 0]

    def share_of(k):
        o = chunks[k][0]
        return far_share[:, o - 1] if o else near_share[:, 0]

    def start_rows(k, *after):
        o, halves = chunks[k]
        own, part_x, part_y, across_a, across_b = partial_sums(
            me, sames[o], others[o], slots_of(k), *weights, after, halves, k > 0
        )
        sums[k] = own
        adds[k] = [part_x, part_y, swap(across_a, "dp", 1), swap(across_b, "dp", 2)]
        return own

    def move(k, r, *after, block=None):
        outs = between(adds.get(k), got.get(r), block, after, k != 0 and r != 0)
        if k in adds:
            sums[k] = sums[k], swap(outs[0], "dp", 1), swap(outs[1], "dp", 2)
        if r in got:
            at = 2 if k in adds else 0
            relayed[r] = swap(outs[at], "dp", 1), swap(outs[at + 1], "dp", 2)
        if block is not None:
            return outs[0], outs[-1], swap(outs[-1], "expert", 1)
        return outs[0]

    def turn_rows(k, *after):
        halves = chunks[k][1]
        first = 2 * member + halves[0]
        own_slot = lax.dynamic_slice_in_dim(slots_of(k), first, len(halves), 0)
        own_share = lax.dynamic_slice_in_dim(share_of(k), first, len(halves), 0)
        expert = (mine * per_device + first).astype(jnp.int32).reshape(1)
        sent[k] = middle(expert, *sums[k], own_slot, own_share, after, k > 0)
        got[k] = [swap(sent[k], "dp", 1), swap(sent[k], "dp", 2)]
        return sent[k]

    def finish_rows(k, *after):
        o, halves = chunks[k]
        given = (sent[k], *got[k], *relayed[k])
        same, other = combine(me, given, slots_of(k), *weights, after, halves)
        blocks[k] = [same, other]
        return same

    after = start_rows(0, after)
    after = move(0, None, after)
    after = turn_rows(0, after, far_slots, far_share)
    after, sames[3], others[3] = move(None, 0, after, block=arriving)
    sames[2] = swap(sames[3], "expert", 2)
    after = start_rows(1, after, *relayed[0])
    after, sames[2], others[2] = move(1, None, after, block=sames[2])
    after = start_rows(2, after)
    after = turn_rows(1, after)
    after = finish_rows(0, after)
    after, sames[1], others[1] = move(2, 1, after, block=sames[1])
    after = start_rows(3, after)
    after = turn_rows(2, after, *relayed[1])
    after = finish_rows(1, after)
    after, _, other = move(3, 2, after, block=blocks[1][1])
    after = start_rows(4, after)
    (after,) = add_up([blocks[1][0], other], 1, after, *relayed[2])
    hop = swap(after, "expert", 2)
    after = turn_rows(3, after, *adds[4][2:])
    after = finish_rows(2, after)
    after, _, other = move(4, 3, after, hop, block=blocks[2][1])
    after, second = add_up([blocks[2][0], other, hop], 2, after)
    far_low, far_high = swap(after, "expert", 4), swap(second, "expert", 4)
    after = finish_rows(3, second)
    after = turn_rows(4, after, far_low)
    after, _, other = move(None, None, after, block=blocks[3][1])
    (after,) = add_up([blocks[3][0], other], 1, after)
    near_back = swap(after, "expert", 2)
    after = move(None, 4, after)
    after = finish_rows(4, after)
    blocks[0][1] = swap(blocks[0][1], "expert", 1)
    _, _, blocks[4][1] = move(
        None, None, after, far_high, near_back, blocks[0][1], block=blocks[4][1]
    )
    far_back = jnp.concatenate([far_low, far_high], axis=0)
    total = sum(t.astype(jnp.float32) for t in (*blocks[0], *blocks[4], near_back, far_back))
    grads = total[:, 2 * features : 2 * features + EXPERTS] + total[:, 2 * features + EXPERTS :]
    hit = routes[:, :, None] == jnp.arange(EXPERTS, dtype=jnp.int32)
    gate_grad = jnp.sum(jnp.where(hit, grads[:, None, :], 0.0), axis=2)
    total = total[:, : 2 * features].astype(jnp.bfloat16)
    return total[:, :features], total[:, features:], gate_grad


def on_device(
    tokens, gate_weight, up_weight, down_weight, routes, gate_levels, log_ratio, cotangent
):
    local_tokens = tokens.shape[0]
    feature_slice = tokens.shape[1]
    hidden = gate_weight.shape[2]
    per_device = gate_weight.shape[0]
    peer_count = lax.axis_size("expert")
    slots_total = EXPERTS * CAP
    pick_ids = routes.reshape(-1)
    onehot_table = (pick_ids[:, None] == jnp.arange(EXPERTS, dtype=jnp.int32)[None, :]).astype(
        jnp.int32
    )
    earlier = jnp.cumsum(onehot_table, axis=0) - onehot_table
    position = jnp.sum(earlier * onehot_table, axis=1)
    target = pick_ids * CAP + position

    def pack_rows(values):
        packed = jnp.zeros((slots_total, feature_slice), jnp.bfloat16).at[target].set(values)
        return packed.reshape(peer_count, per_device * CAP, feature_slice)

    received = lax.all_to_all(
        pack_rows(jnp.repeat(tokens, TOPK, axis=0)),
        "expert",
        split_axis=0,
        concat_axis=0,
        tiled=True,
    )
    arrived = received.reshape(peer_count, per_device, CAP, feature_slice)
    gate_part = jnp.einsum(
        "sjcd,jdf->sjcf", arrived, gate_weight, preferred_element_type=jnp.float32
    ).reshape(-1, hidden)
    up_part = jnp.einsum(
        "sjcd,jdf->sjcf", arrived, up_weight, preferred_element_type=jnp.float32
    ).reshape(-1, hidden)
    gate_share, up_share = (
        lax.psum_scatter(gate_part, "dp", scatter_dimension=0, tiled=True),
        lax.psum_scatter(up_part, "dp", scatter_dimension=0, tiled=True),
    )
    activated = lax.all_gather(
        (jax.nn.silu(gate_share) * up_share).astype(jnp.bfloat16), "dp", axis=0, tiled=True
    )
    expert_out = jnp.einsum(
        "sjcf,jfd->sjcd",
        activated.reshape(peer_count, per_device, CAP, hidden),
        down_weight,
        preferred_element_type=jnp.float32,
    ).astype(jnp.bfloat16)
    returned = lax.all_to_all(
        expert_out.reshape(peer_count, per_device * CAP, feature_slice),
        "expert",
        split_axis=0,
        concat_axis=0,
        tiled=True,
    )
    picked = (
        returned.reshape(slots_total, feature_slice)[target]
        .reshape(local_tokens, TOPK, feature_slice)
        .astype(jnp.float32)
    )
    levels = gate_levels.astype(jnp.float32)
    fractions = levels / jnp.sum(levels, axis=1, keepdims=True)
    mixed_out = jnp.sum(fractions[:, :, None] * picked, axis=1).astype(jnp.bfloat16)
    ratio_weight = jnp.minimum(jnp.exp(log_ratio), clip_ratio)
    weighted = (ratio_weight[:, None] * cotangent.astype(jnp.float32)).astype(jnp.bfloat16)
    weighted_wide = weighted.astype(jnp.float32)[:, None, :]
    gate_grad = lax.psum(jnp.sum(weighted_wide * picked, axis=2), "dp")
    pick_grad = (
        (fractions[:, :, None] * weighted_wide).astype(jnp.bfloat16).reshape(-1, feature_slice)
    )
    back_rows = lax.all_to_all(
        pack_rows(pick_grad), "expert", split_axis=0, concat_axis=0, tiled=True
    )
    back_rows = back_rows.reshape(peer_count, per_device, CAP, feature_slice)
    hidden_part = jnp.einsum(
        "sjcd,jfd->sjcf", back_rows, down_weight, preferred_element_type=jnp.float32
    ).reshape(-1, hidden)
    hidden_grad = lax.psum_scatter(hidden_part, "dp", scatter_dimension=0, tiled=True)
    sigmoid_gate = jax.nn.sigmoid(gate_share)
    gate_back = (
        hidden_grad * up_share * sigmoid_gate * (1.0 + gate_share * (1.0 - sigmoid_gate))
    ).astype(jnp.bfloat16)
    up_back = (hidden_grad * gate_share * sigmoid_gate).astype(jnp.bfloat16)
    gate_rows, up_rows = (
        lax.all_gather(gate_back, "dp", axis=0, tiled=True),
        lax.all_gather(up_back, "dp", axis=0, tiled=True),
    )
    gate_rows = gate_rows.reshape(peer_count, per_device, CAP, hidden)
    up_rows = up_rows.reshape(peer_count, per_device, CAP, hidden)
    input_part = jnp.einsum(
        "sjcf,jdf->sjcd", gate_rows, gate_weight, preferred_element_type=jnp.float32
    )
    input_part = (
        input_part
        + jnp.einsum("sjcf,jdf->sjcd", up_rows, up_weight, preferred_element_type=jnp.float32)
    ).astype(jnp.bfloat16)
    input_back = lax.all_to_all(
        input_part.reshape(peer_count, per_device * CAP, feature_slice),
        "expert",
        split_axis=0,
        concat_axis=0,
        tiled=True,
    )
    back_picked = input_back.reshape(slots_total, feature_slice)[target].reshape(
        local_tokens, TOPK, feature_slice
    )
    token_grad = jnp.sum(back_picked.astype(jnp.float32), axis=1).astype(jnp.bfloat16)
    return (mixed_out, token_grad, gate_grad)


def solution(mesh):
    in_specs = (
        P("expert", "dp"),
        P("expert", "dp", None),
        P("expert", "dp", None),
        P("expert", None, "dp"),
        P("expert", None),
        P("expert", None),
        P("expert"),
        P("expert", "dp"),
    )
    out_specs = (P("expert", "dp"), P("expert", "dp"), P("expert", None))
    fits = mesh.shape["dp"] == 4 and mesh.shape["expert"] == 8
    return jax.shard_map(
        grouped if fits else on_device,
        mesh=mesh, in_specs=in_specs, out_specs=out_specs, check_vma=False,
    )
```

```python
import functools
import jax
import jax.numpy as jnp
from jax import lax
from jax.experimental import pallas as pl
from jax.experimental.pallas import tpu as pltpu
from jax.sharding import PartitionSpec as P

EXPERTS = 64
TOPK = 8
CAP = 40
VMEM_BYTES = 50 * 1024 * 1024


def moves(ample):
    count = 400_000_000 if ample else 1000
    return pl.CostEstimate(flops=count, bytes_accessed=count, transcendentals=0)


clip_ratio = 2.0


def dot_nn(a, b):
    return lax.dot_general(a, b, (((1,), (0,)), ((), ())), preferred_element_type=jnp.float32)


def dot_nt(a, b):
    return lax.dot_general(a, b, (((1,), (1,)), ((), ())), preferred_element_type=jnp.float32)


def dot_tn(a, b):
    return lax.dot_general(a, b, (((0,), (0,)), ((), ())), preferred_element_type=jnp.float32)


def one_hot(slots_ref, rows):
    slots = slots_ref[0]
    return slots == lax.broadcasted_iota(jnp.int32, (rows, slots.shape[-1]), 0)


def whole(shape):
    return pl.BlockSpec(shape, lambda g, me: (0,) * len(shape))


def expert_block(shape, halves):
    count = len(halves)
    return pl.BlockSpec(
        (1,) + shape,
        lambda g, me: (2 * ((g // count) ^ me[0]) + (halves[0] + g % count), 0, 0),
    )


def partial_kernel(count, me, same, other, slots, w_gate, w_up, w_down, *rest):
    own, part_x, part_y, across_a, across_b = rest[-5:]
    step = pl.program_id(0)
    part, half = step // count, step % count
    tokens, width = same.shape
    rows = own.shape[1]
    hidden = w_gate.shape[2]
    cut = across_a.shape[2]
    pick = jnp.where(one_hot(slots, rows), 1.0, 0.0).astype(jnp.bfloat16)
    taken = dot_nn(pick[:, :tokens], same[...]) + dot_nn(pick[:, tokens:], other[...])
    taken = taken.astype(jnp.bfloat16)
    features = width // 2
    gate = dot_nn(taken[:, :features], w_gate[0]).astype(jnp.bfloat16)
    up = dot_nn(taken[:, :features], w_up[0]).astype(jnp.bfloat16)
    back = dot_nt(taken[:, features:], w_down[0]).astype(jnp.bfloat16)
    for v, ref in enumerate((own, part_x, part_y)):
        @pl.when(part == v)
        def _():
            ref[half, :, pl.ds(0, hidden)] = gate
            ref[half, :, pl.ds(hidden, hidden)] = up
            ref[half, :, pl.ds(2 * hidden, hidden)] = back

    @pl.when(part == 3)
    def _():
        across_a[half, :, pl.ds(0, hidden)] = gate
        across_a[half, :, pl.ds(hidden, cut - hidden)] = up[:, : cut - hidden]
        across_b[half, :, pl.ds(0, cut - hidden)] = up[:, cut - hidden :]
        across_b[half, :, pl.ds(cut - hidden, hidden)] = back


def partial_sums(me, same, other, slots, w_gate, w_up, w_down, after, halves, ample):
    count = len(halves)
    features, hidden = w_gate.shape[1:]
    rows, cols = 2 * CAP, 3 * hidden
    full = jax.ShapeDtypeStruct((count, rows, cols), jnp.bfloat16)
    cut = jax.ShapeDtypeStruct((count, rows, cols // 2), jnp.bfloat16)
    outs = (full, full, full, cut, cut)
    steps = 4 * count
    return pl.pallas_call(
        functools.partial(partial_kernel, count),
        grid_spec=pltpu.PrefetchScalarGridSpec(
            num_scalar_prefetch=1,
            grid=(steps,),
            in_specs=[
                whole(same.shape),
                whole(other.shape),
                expert_block(slots.shape[1:], halves),
                expert_block((features, hidden), halves),
                expert_block((features, hidden), halves),
                expert_block((hidden, features), halves),
                *[pl.BlockSpec(memory_space=pl.ANY)] * len(after),
            ],
            out_specs=[whole(o.shape) for o in outs],
        ),
        out_shape=outs,
        compiler_params=pltpu.CompilerParams(vmem_limit_bytes=VMEM_BYTES),
        cost_estimate=moves(ample),
    )(me, same, other, slots, w_gate, w_up, w_down, *after)


def middle_kernel(me, own, from_x, from_y, slots, share, *rest):
    out = rest[-1]
    count, rows, cols = own.shape
    hidden = cols // 3
    half = hidden // 2
    extra = 2 * EXPERTS
    for h in range(count):
        def total(lo):
            cut = pl.ds(lo, half)
            return (
                own[h, :, cut].astype(jnp.float32)
                + from_x[h, :, cut].astype(jnp.float32)
                + from_y[h, :, cut].astype(jnp.float32)
            )
        hot = one_hot(slots.at[pl.ds(h, 1)], rows)
        fraction = jnp.sum(jnp.where(hot, share[h], 0.0), axis=1, keepdims=True)
        grads = jnp.zeros((rows, 1), jnp.float32)
        for side in range(2):
            lo = side * half
            gate, up, back = total(lo), total(hidden + lo), total(2 * hidden + lo)
            sig = 1.0 / (1.0 + jnp.exp(-gate))
            silu = gate * sig
            act = silu * up
            grads = grads + jnp.sum(act * back, axis=1, keepdims=True)
            hidden_grad = back * fraction
            act_out = (act * fraction).astype(jnp.bfloat16)
            gate_out = (hidden_grad * up * sig * (1.0 + gate * (1.0 - sig))).astype(jnp.bfloat16)
            up_out = (hidden_grad * silu).astype(jnp.bfloat16)
            out[h, :, pl.ds(lo, half)] = act_out
            out[h, :, pl.ds(hidden + side * (half + extra), half)] = gate_out
            out[h, :, pl.ds(2 * hidden + extra + lo, half)] = up_out
        lane = lax.broadcasted_iota(jnp.int32, (rows, extra), 1)
        high = grads.astype(jnp.bfloat16).astype(jnp.float32)
        spread = jnp.where(lane == me[0] + h, high, 0.0)
        spread = jnp.where(lane == me[0] + h + EXPERTS, grads - high, spread)
        out[h, :, pl.ds(cols // 2, extra)] = spread.astype(jnp.bfloat16)


def at_once(shape):
    return pl.BlockSpec(shape, lambda g: (0,) * len(shape))


def middle(first, own, from_x, from_y, slots, share, after, ample):
    count, rows, cols = own.shape
    out = jax.ShapeDtypeStruct((count, rows, cols + 2 * EXPERTS), jnp.bfloat16)
    return pl.pallas_call(
        middle_kernel,
        grid=(1,),
        out_shape=out,
        in_specs=[pl.BlockSpec(memory_space=pltpu.SMEM)]
        + [at_once(a.shape) for a in (own, from_x, from_y, slots, share)]
        + [pl.BlockSpec(memory_space=pl.ANY)] * len(after),
        out_specs=at_once(out.shape),
        compiler_params=pltpu.CompilerParams(vmem_limit_bytes=VMEM_BYTES),
        cost_estimate=moves(ample),
    )(first, own, from_x, from_y, slots, share, *after)


def between_kernel(waits, adds, relays, passes, *refs):
    count = 4 * adds + 2 * relays + passes
    ins, outs = list(refs[:count]), list(refs[count + waits :])
    if adds:
        part_x, part_y, given_a, given_b = ins[:4]
        to_x, to_y = outs[:2]
        cut = given_a.shape[2]
        low, high = pl.ds(0, cut), pl.ds(cut, cut)
        to_x[:, :, low] = part_x[:, :, low]
        to_x[:, :, high] = (
            part_x[:, :, high].astype(jnp.float32) + given_b[...].astype(jnp.float32)
        ).astype(jnp.bfloat16)
        to_y[:, :, low] = (
            part_y[:, :, low].astype(jnp.float32) + given_a[...].astype(jnp.float32)
        ).astype(jnp.bfloat16)
        to_y[:, :, high] = part_y[:, :, high]
        ins, outs = ins[4:], outs[2:]
    if relays:
        rows_x, rows_y = ins[:2]
        out_a, out_b = outs[:2]
        cut = out_a.shape[2]
        out_a[...] = rows_y[:, :, pl.ds(0, cut)]
        out_b[...] = rows_x[:, :, pl.ds(cut, out_b.shape[2])]
        ins, outs = ins[2:], outs[2:]
    if passes:
        outs[0][...] = ins[0][...]


def between(add, relay, block, after, ample):
    ins, outs = [], []
    if add is not None:
        ins += add
        outs += [add[0].shape, add[1].shape]
    if relay is not None:
        ins += relay
        count, rows, width = relay[0].shape
        cols = (width - 2 * EXPERTS) // 2
        outs += [(count, rows, cols + 2 * EXPERTS), (count, rows, cols)]
    if block is not None:
        ins += [block]
        outs += [block.shape]
    given = [int(a is not None) for a in (add, relay, block)]
    return pl.pallas_call(
        functools.partial(between_kernel, len(after), *given),
        grid=(1,),
        out_shape=[jax.ShapeDtypeStruct(o, jnp.bfloat16) for o in outs],
        in_specs=[at_once(i.shape) for i in ins]
        + [pl.BlockSpec(memory_space=pl.ANY)] * len(after),
        out_specs=[at_once(o) for o in outs],
        compiler_params=pltpu.CompilerParams(vmem_limit_bytes=VMEM_BYTES),
        cost_estimate=moves(ample),
    )(*ins, *after)


def add_up_kernel(count, waits, *refs):
    ins, outs = refs[:count], refs[count + waits :]
    for n, out in enumerate(outs):
        cut = pl.ds(n * out.shape[0], out.shape[0])
        total = ins[0][cut, :].astype(jnp.float32)
        for ref in ins[1:]:
            total = total + ref[cut, :].astype(jnp.float32)
        out[...] = total.astype(jnp.bfloat16)


def add_up(blocks, splits, *after):
    rows, width = blocks[0].shape
    out = jax.ShapeDtypeStruct((rows // splits, width), jnp.bfloat16)
    return pl.pallas_call(
        functools.partial(add_up_kernel, len(blocks), len(after)),
        grid=(1,),
        out_shape=[out] * splits,
        in_specs=[at_once((rows, width))] * len(blocks)
        + [pl.BlockSpec(memory_space=pl.ANY)] * len(after),
        out_specs=[at_once(out.shape)] * splits,
        compiler_params=pltpu.CompilerParams(vmem_limit_bytes=VMEM_BYTES),
        cost_estimate=moves(True),
    )(*blocks, *after)


def combine_kernel(count, waits, me, *refs):
    across_a, across_b = refs[3:5]
    slots, w_gate, w_up, w_down = refs[5:9]
    same, other, rows_in, hots, outs = refs[9 + waits :]
    step = pl.program_id(0)
    part, half = step // count, step % count
    rows, cols = rows_in.shape[0], across_b.shape[2]
    extra = pl.ds(cols, 2 * EXPERTS)
    hidden = w_gate.shape[2]
    features = w_gate.shape[1]
    at = pl.ds(pl.multiple_of(step * rows, 16), rows)
    for v in range(4):
        @pl.when(part == v)
        def _():
            left = refs[v] if v < 3 else across_a
            rows_in[:, pl.ds(0, cols)] = left[half, :, pl.ds(0, cols)]
            outs[at, pl.ds(2 * features, 2 * EXPERTS)] = left[half, :, extra]
            if v < 3:
                rows_in[:, pl.ds(cols, cols)] = left[half, :, pl.ds(cols + 2 * EXPERTS, cols)]
            else:
                rows_in[:, pl.ds(cols, cols)] = across_b[half]
    outs[at, pl.ds(0, features)] = dot_nn(rows_in[:, pl.ds(0, hidden)], w_down[0]).astype(jnp.bfloat16)
    outs[at, pl.ds(features, features)] = (
        dot_nt(rows_in[:, pl.ds(hidden, hidden)], w_gate[0])
        + dot_nt(rows_in[:, pl.ds(2 * hidden, hidden)], w_up[0])
    ).astype(jnp.bfloat16)
    hots[at, :] = jnp.where(one_hot(slots, rows), 1.0, 0.0).astype(jnp.bfloat16)

    @pl.when(step == pl.num_programs(0) - 1)
    def _():
        tokens, width = same.shape
        for ref, lo in ((same, 0), (other, tokens)):
            ref[...] = dot_tn(hots[:, pl.ds(lo, tokens)], outs[...]).astype(jnp.bfloat16)


def combine(me, given, slots, w_gate, w_up, w_down, after, halves, ample=True):
    count = len(halves)
    features, hidden = w_gate.shape[1:]
    rows = 2 * CAP
    tokens = slots.shape[2] // 2
    steps = 4 * count
    width = 2 * features + 2 * EXPERTS
    out = jax.ShapeDtypeStruct((tokens, width), jnp.bfloat16)
    return pl.pallas_call(
        functools.partial(combine_kernel, count, len(after)),
        grid_spec=pltpu.PrefetchScalarGridSpec(
            num_scalar_prefetch=1,
            grid=(steps,),
            in_specs=[whole(a.shape) for a in given]
            + [
                expert_block(slots.shape[1:], halves),
                expert_block((features, hidden), halves),
                expert_block((features, hidden), halves),
                expert_block((hidden, features), halves),
                *[pl.BlockSpec(memory_space=pl.ANY)] * len(after),
            ],
            out_specs=[whole(out.shape)] * 2,
            scratch_shapes=[
                pltpu.VMEM((rows, 3 * hidden), jnp.bfloat16),
                pltpu.VMEM((steps * rows, 2 * tokens), jnp.bfloat16),
                pltpu.VMEM((steps * rows, width), jnp.bfloat16),
            ],
        ),
        out_shape=(out, out),
        compiler_params=pltpu.CompilerParams(vmem_limit_bytes=VMEM_BYTES),
        cost_estimate=moves(ample),
    )(me, *given, slots, w_gate, w_up, w_down, *after)


def swap(value, axis, bits):
    count = lax.axis_size(axis)
    return lax.ppermute(value, axis, [(n, n ^ bits) for n in range(count)])


def grouped(tokens, gate_weight, up_weight, down_weight, routes, gate_levels, log_ratio, cotangent):
    block, features = tokens.shape
    per_device = gate_weight.shape[0]
    peers = lax.axis_size("expert")
    chips = peers // 2
    mine = lax.axis_index("expert")
    member = lax.axis_index("dp")
    me = member.astype(jnp.int32).reshape(1)

    ratio_weight = jnp.minimum(jnp.exp(log_ratio), clip_ratio)
    weighted = (ratio_weight[:, None] * cotangent.astype(jnp.float32)).astype(jnp.bfloat16)
    payload = jnp.concatenate([tokens, weighted], axis=1)
    arriving = swap(payload, "expert", 6)
    sames = {0: payload, 1: swap(payload, "expert", 2)}
    others = {0: swap(payload, "expert", 1)}

    local = mine * per_device + jnp.arange(per_device, dtype=jnp.int32)
    tri = (jnp.arange(block)[:, None] < jnp.arange(block)[None, :]).astype(jnp.bfloat16)

    def placed(picks):
        levels = picks[:, 1].astype(jnp.float32)
        fractions = levels / jnp.sum(levels, axis=1, keepdims=True)
        named = picks[:, 0][None] == local[:, None, None, None]
        share = jnp.sum(jnp.where(named, fractions[None], 0.0), axis=2)
        chosen = jnp.any(named, axis=2)
        place = jnp.einsum(
            "jst,tu->jsu", chosen.astype(jnp.bfloat16), tri, preferred_element_type=jnp.float32
        ).astype(jnp.int32)
        place = place + (jnp.arange(picks.shape[0], dtype=jnp.int32) % 2 * CAP)[None, :, None]
        slots = jnp.where(chosen, place, -1)
        pairs = (per_device, picks.shape[0] // 2, 1, 2 * block)
        return slots.reshape(pairs), share.reshape(pairs)

    picks = jnp.stack([routes.T, gate_levels.T])
    near = jnp.stack([picks, swap(picks, "expert", 1)])
    away = jnp.stack([swap(picks, "expert", 2 * o) for o in range(1, chips)])
    far = jnp.stack([away, swap(away, "expert", 1)], axis=1).reshape(-1, *picks.shape)
    near_slots, near_share = placed(near)
    far_slots, far_share = placed(far)

    weights = (gate_weight, up_weight, down_weight)
    chunks = [(0, (0,)), (3, (0, 1)), (2, (0, 1)), (1, (0, 1)), (0, (1,))]
    sums, adds, sent, got, relayed, blocks = {}, {}, {}, {}, {}, {}
    after = near_slots

    def slots_of(k):
        o = chunks[k][0]
        return far_slots[:, o - 1] if o else near_slots[:, 0]

    def share_of(k):
        o = chunks[k][0]
        return far_share[:, o - 1] if o else near_share[:, 0]

    def start_rows(k, *after):
        o, halves = chunks[k]
        own, part_x, part_y, across_a, across_b = partial_sums(
            me, sames[o], others[o], slots_of(k), *weights, after, halves, k > 0
        )
        sums[k] = own
        adds[k] = [part_x, part_y, swap(across_a, "dp", 1), swap(across_b, "dp", 2)]
        return own

    def move(k, r, *after, block=None):
        outs = between(adds.get(k), got.get(r), block, after, k != 0 and r != 0)
        if k in adds:
            sums[k] = sums[k], swap(outs[0], "dp", 1), swap(outs[1], "dp", 2)
        if r in got:
            at = 2 if k in adds else 0
            relayed[r] = swap(outs[at], "dp", 1), swap(outs[at + 1], "dp", 2)
        if block is not None:
            return outs[0], outs[-1], swap(outs[-1], "expert", 1)
        return outs[0]

    def turn_rows(k, *after):
        halves = chunks[k][1]
        first = 2 * member + halves[0]
        own_slot = lax.dynamic_slice_in_dim(slots_of(k), first, len(halves), 0)
        own_share = lax.dynamic_slice_in_dim(share_of(k), first, len(halves), 0)
        expert = (mine * per_device + first).astype(jnp.int32).reshape(1)
        sent[k] = middle(expert, *sums[k], own_slot, own_share, after, k > 0)
        got[k] = [swap(sent[k], "dp", 1), swap(sent[k], "dp", 2)]
        return sent[k]

    def finish_rows(k, *after):
        o, halves = chunks[k]
        given = (sent[k], *got[k], *relayed[k])
        same, other = combine(me, given, slots_of(k), *weights, after, halves)
        blocks[k] = [same, other]
        return same

    after = start_rows(0, after)
    after = move(0, None, after)
    after = turn_rows(0, after, far_slots, far_share)
    after, sames[3], others[3] = move(None, 0, after, block=arriving)
    sames[2] = swap(sames[3], "expert", 2)
    after = start_rows(1, after)
    after, sames[2], others[2] = move(1, None, after, block=sames[2])
    after = start_rows(2, after)
    after = turn_rows(1, after, *relayed[0])
    after = finish_rows(0, after)
    after, sames[1], others[1] = move(2, 1, after, block=sames[1])
    after = start_rows(3, after)
    after = turn_rows(2, after, *relayed[1])
    after = finish_rows(1, after)
    after, _, other = move(3, 2, after, block=blocks[1][1])
    after = start_rows(4, after)
    (after,) = add_up([blocks[1][0], other], 1, after, *relayed[2])
    hop = swap(after, "expert", 2)
    after = turn_rows(3, after, *adds[4][2:])
    after = finish_rows(2, after)
    after, _, other = move(4, 3, after, hop, block=blocks[2][1])
    after, second = add_up([blocks[2][0], other, hop], 2, after)
    far_low, far_high = swap(after, "expert", 4), swap(second, "expert", 4)
    after = finish_rows(3, second)
    after = turn_rows(4, after, far_low)
    after, _, other = move(None, None, after, block=blocks[3][1])
    (after,) = add_up([blocks[3][0], other], 1, after)
    near_back = swap(after, "expert", 2)
    after = move(None, 4, after)
    after = finish_rows(4, after)
    blocks[0][1] = swap(blocks[0][1], "expert", 1)
    _, _, blocks[4][1] = move(
        None, None, after, far_high, near_back, blocks[0][1], block=blocks[4][1]
    )
    far_back = jnp.concatenate([far_low, far_high], axis=0)
    total = sum(t.astype(jnp.float32) for t in (*blocks[0], *blocks[4], near_back, far_back))
    grads = total[:, 2 * features : 2 * features + EXPERTS] + total[:, 2 * features + EXPERTS :]
    hit = routes[:, :, None] == jnp.arange(EXPERTS, dtype=jnp.int32)
    gate_grad = jnp.sum(jnp.where(hit, grads[:, None, :], 0.0), axis=2)
    total = total[:, : 2 * features].astype(jnp.bfloat16)
    return total[:, :features], total[:, features:], gate_grad


def on_device(
    tokens, gate_weight, up_weight, down_weight, routes, gate_levels, log_ratio, cotangent
):
    local_tokens = tokens.shape[0]
    feature_slice = tokens.shape[1]
    hidden = gate_weight.shape[2]
    per_device = gate_weight.shape[0]
    peer_count = lax.axis_size("expert")
    slots_total = EXPERTS * CAP
    pick_ids = routes.reshape(-1)
    onehot_table = (pick_ids[:, None] == jnp.arange(EXPERTS, dtype=jnp.int32)[None, :]).astype(
        jnp.int32
    )
    earlier = jnp.cumsum(onehot_table, axis=0) - onehot_table
    position = jnp.sum(earlier * onehot_table, axis=1)
    target = pick_ids * CAP + position

    def pack_rows(values):
        packed = jnp.zeros((slots_total, feature_slice), jnp.bfloat16).at[target].set(values)
        return packed.reshape(peer_count, per_device * CAP, feature_slice)

    received = lax.all_to_all(
        pack_rows(jnp.repeat(tokens, TOPK, axis=0)),
        "expert",
        split_axis=0,
        concat_axis=0,
        tiled=True,
    )
    arrived = received.reshape(peer_count, per_device, CAP, feature_slice)
    gate_part = jnp.einsum(
        "sjcd,jdf->sjcf", arrived, gate_weight, preferred_element_type=jnp.float32
    ).reshape(-1, hidden)
    up_part = jnp.einsum(
        "sjcd,jdf->sjcf", arrived, up_weight, preferred_element_type=jnp.float32
    ).reshape(-1, hidden)
    gate_share, up_share = (
        lax.psum_scatter(gate_part, "dp", scatter_dimension=0, tiled=True),
        lax.psum_scatter(up_part, "dp", scatter_dimension=0, tiled=True),
    )
    activated = lax.all_gather(
        (jax.nn.silu(gate_share) * up_share).astype(jnp.bfloat16), "dp", axis=0, tiled=True
    )
    expert_out = jnp.einsum(
        "sjcf,jfd->sjcd",
        activated.reshape(peer_count, per_device, CAP, hidden),
        down_weight,
        preferred_element_type=jnp.float32,
    ).astype(jnp.bfloat16)
    returned = lax.all_to_all(
        expert_out.reshape(peer_count, per_device * CAP, feature_slice),
        "expert",
        split_axis=0,
        concat_axis=0,
        tiled=True,
    )
    picked = (
        returned.reshape(slots_total, feature_slice)[target]
        .reshape(local_tokens, TOPK, feature_slice)
        .astype(jnp.float32)
    )
    levels = gate_levels.astype(jnp.float32)
    fractions = levels / jnp.sum(levels, axis=1, keepdims=True)
    mixed_out = jnp.sum(fractions[:, :, None] * picked, axis=1).astype(jnp.bfloat16)
    ratio_weight = jnp.minimum(jnp.exp(log_ratio), clip_ratio)
    weighted = (ratio_weight[:, None] * cotangent.astype(jnp.float32)).astype(jnp.bfloat16)
    weighted_wide = weighted.astype(jnp.float32)[:, None, :]
    gate_grad = lax.psum(jnp.sum(weighted_wide * picked, axis=2), "dp")
    pick_grad = (
        (fractions[:, :, None] * weighted_wide).astype(jnp.bfloat16).reshape(-1, feature_slice)
    )
    back_rows = lax.all_to_all(
        pack_rows(pick_grad), "expert", split_axis=0, concat_axis=0, tiled=True
    )
    back_rows = back_rows.reshape(peer_count, per_device, CAP, feature_slice)
    hidden_part = jnp.einsum(
        "sjcd,jfd->sjcf", back_rows, down_weight, preferred_element_type=jnp.float32
    ).reshape(-1, hidden)
    hidden_grad = lax.psum_scatter(hidden_part, "dp", scatter_dimension=0, tiled=True)
    sigmoid_gate = jax.nn.sigmoid(gate_share)
    gate_back = (
        hidden_grad * up_share * sigmoid_gate * (1.0 + gate_share * (1.0 - sigmoid_gate))
    ).astype(jnp.bfloat16)
    up_back = (hidden_grad * gate_share * sigmoid_gate).astype(jnp.bfloat16)
    gate_rows, up_rows = (
        lax.all_gather(gate_back, "dp", axis=0, tiled=True),
        lax.all_gather(up_back, "dp", axis=0, tiled=True),
    )
    gate_rows = gate_rows.reshape(peer_count, per_device, CAP, hidden)
    up_rows = up_rows.reshape(peer_count, per_device, CAP, hidden)
    input_part = jnp.einsum(
        "sjcf,jdf->sjcd", gate_rows, gate_weight, preferred_element_type=jnp.float32
    )
    input_part = (
        input_part
        + jnp.einsum("sjcf,jdf->sjcd", up_rows, up_weight, preferred_element_type=jnp.float32)
    ).astype(jnp.bfloat16)
    input_back = lax.all_to_all(
        input_part.reshape(peer_count, per_device * CAP, feature_slice),
        "expert",
        split_axis=0,
        concat_axis=0,
        tiled=True,
    )
    back_picked = input_back.reshape(slots_total, feature_slice)[target].reshape(
        local_tokens, TOPK, feature_slice
    )
    token_grad = jnp.sum(back_picked.astype(jnp.float32), axis=1).astype(jnp.bfloat16)
    return (mixed_out, token_grad, gate_grad)


def solution(mesh):
    in_specs = (
        P("expert", "dp"),
        P("expert", "dp", None),
        P("expert", "dp", None),
        P("expert", None, "dp"),
        P("expert", None),
        P("expert", None),
        P("expert"),
        P("expert", "dp"),
    )
    out_specs = (P("expert", "dp"), P("expert", "dp"), P("expert", None))
    fits = mesh.shape["dp"] == 4 and mesh.shape["expert"] == 8
    return jax.shard_map(
        grouped if fits else on_device,
        mesh=mesh, in_specs=in_specs, out_specs=out_specs, check_vma=False,
    )
```

```python
import functools
import jax
import jax.numpy as jnp
from jax import lax
from jax.experimental import pallas as pl
from jax.experimental.pallas import tpu as pltpu
from jax.sharding import PartitionSpec as P

EXPERTS = 64
TOPK = 8
CAP = 40
VMEM_BYTES = 40 * 1024 * 1024


def moves(ample):
    count = 400_000_000 if ample else 1000
    return pl.CostEstimate(flops=count, bytes_accessed=count, transcendentals=0)


clip_ratio = 2.0


def dot_nn(a, b):
    return lax.dot_general(a, b, (((1,), (0,)), ((), ())), preferred_element_type=jnp.float32)


def dot_nt(a, b):
    return lax.dot_general(a, b, (((1,), (1,)), ((), ())), preferred_element_type=jnp.float32)


def dot_tn(a, b):
    return lax.dot_general(a, b, (((0,), (0,)), ((), ())), preferred_element_type=jnp.float32)


def one_hot(slots_ref, rows):
    slots = slots_ref[0]
    return slots == lax.broadcasted_iota(jnp.int32, (rows, slots.shape[-1]), 0)


def whole(shape):
    return pl.BlockSpec(shape, lambda g, me: (0,) * len(shape))


def expert_block(shape, halves):
    count = len(halves)
    return pl.BlockSpec(
        (1,) + shape,
        lambda g, me: (2 * ((g // count) ^ me[0]) + (halves[0] + g % count), 0, 0),
    )


def partial_kernel(count, me, same, other, slots, w_gate, w_up, w_down, *rest):
    own, part_x, part_y, across_a, across_b = rest[-5:]
    step = pl.program_id(0)
    part, half = step // count, step % count
    tokens, width = same.shape
    rows = own.shape[1]
    hidden = w_gate.shape[2]
    cut = across_a.shape[2]
    pick = jnp.where(one_hot(slots, rows), 1.0, 0.0).astype(jnp.bfloat16)
    taken = dot_nn(pick[:, :tokens], same[...]) + dot_nn(pick[:, tokens:], other[...])
    taken = taken.astype(jnp.bfloat16)
    features = width // 2
    gate = dot_nn(taken[:, :features], w_gate[0]).astype(jnp.bfloat16)
    up = dot_nn(taken[:, :features], w_up[0]).astype(jnp.bfloat16)
    back = dot_nt(taken[:, features:], w_down[0]).astype(jnp.bfloat16)
    for v, ref in enumerate((own, part_x, part_y)):
        @pl.when(part == v)
        def _():
            ref[half, :, pl.ds(0, hidden)] = gate
            ref[half, :, pl.ds(hidden, hidden)] = up
            ref[half, :, pl.ds(2 * hidden, hidden)] = back

    @pl.when(part == 3)
    def _():
        across_a[half, :, pl.ds(0, hidden)] = gate
        across_a[half, :, pl.ds(hidden, cut - hidden)] = up[:, : cut - hidden]
        across_b[half, :, pl.ds(0, cut - hidden)] = up[:, cut - hidden :]
        across_b[half, :, pl.ds(cut - hidden, hidden)] = back


def partial_sums(me, same, other, slots, w_gate, w_up, w_down, after, halves, ample):
    count = len(halves)
    features, hidden = w_gate.shape[1:]
    rows, cols = 2 * CAP, 3 * hidden
    full = jax.ShapeDtypeStruct((count, rows, cols), jnp.bfloat16)
    cut = jax.ShapeDtypeStruct((count, rows, cols // 2), jnp.bfloat16)
    outs = (full, full, full, cut, cut)
    steps = 4 * count
    return pl.pallas_call(
        functools.partial(partial_kernel, count),
        grid_spec=pltpu.PrefetchScalarGridSpec(
            num_scalar_prefetch=1,
            grid=(steps,),
            in_specs=[
                whole(same.shape),
                whole(other.shape),
                expert_block(slots.shape[1:], halves),
                expert_block((features, hidden), halves),
                expert_block((features, hidden), halves),
                expert_block((hidden, features), halves),
                *[pl.BlockSpec(memory_space=pl.ANY)] * len(after),
            ],
            out_specs=[whole(o.shape) for o in outs],
        ),
        out_shape=outs,
        compiler_params=pltpu.CompilerParams(vmem_limit_bytes=VMEM_BYTES),
        cost_estimate=moves(ample),
    )(me, same, other, slots, w_gate, w_up, w_down, *after)


def middle_kernel(me, own, from_x, from_y, slots, share, *rest):
    out = rest[-1]
    count, rows, cols = own.shape
    hidden = cols // 3
    half = hidden // 2
    extra = 2 * EXPERTS
    for h in range(count):
        def total(lo):
            cut = pl.ds(lo, half)
            return (
                own[h, :, cut].astype(jnp.float32)
                + from_x[h, :, cut].astype(jnp.float32)
                + from_y[h, :, cut].astype(jnp.float32)
            )
        hot = one_hot(slots.at[pl.ds(h, 1)], rows)
        fraction = jnp.sum(jnp.where(hot, share[h], 0.0), axis=1, keepdims=True)
        grads = jnp.zeros((rows, 1), jnp.float32)
        for side in range(2):
            lo = side * half
            gate, up, back = total(lo), total(hidden + lo), total(2 * hidden + lo)
            sig = 1.0 / (1.0 + jnp.exp(-gate))
            silu = gate * sig
            act = silu * up
            grads = grads + jnp.sum(act * back, axis=1, keepdims=True)
            hidden_grad = back * fraction
            act_out = (act * fraction).astype(jnp.bfloat16)
            gate_out = (hidden_grad * up * sig * (1.0 + gate * (1.0 - sig))).astype(jnp.bfloat16)
            up_out = (hidden_grad * silu).astype(jnp.bfloat16)
            out[h, :, pl.ds(lo, half)] = act_out
            out[h, :, pl.ds(hidden + side * (half + extra), half)] = gate_out
            out[h, :, pl.ds(2 * hidden + extra + lo, half)] = up_out
        lane = lax.broadcasted_iota(jnp.int32, (rows, extra), 1)
        high = grads.astype(jnp.bfloat16).astype(jnp.float32)
        spread = jnp.where(lane == me[0] + h, high, 0.0)
        spread = jnp.where(lane == me[0] + h + EXPERTS, grads - high, spread)
        out[h, :, pl.ds(cols // 2, extra)] = spread.astype(jnp.bfloat16)


def at_once(shape):
    return pl.BlockSpec(shape, lambda g: (0,) * len(shape))


def middle(first, own, from_x, from_y, slots, share, after, ample):
    count, rows, cols = own.shape
    out = jax.ShapeDtypeStruct((count, rows, cols + 2 * EXPERTS), jnp.bfloat16)
    return pl.pallas_call(
        middle_kernel,
        grid=(1,),
        out_shape=out,
        in_specs=[pl.BlockSpec(memory_space=pltpu.SMEM)]
        + [at_once(a.shape) for a in (own, from_x, from_y, slots, share)]
        + [pl.BlockSpec(memory_space=pl.ANY)] * len(after),
        out_specs=at_once(out.shape),
        compiler_params=pltpu.CompilerParams(vmem_limit_bytes=VMEM_BYTES),
        cost_estimate=moves(ample),
    )(first, own, from_x, from_y, slots, share, *after)


def between_kernel(waits, adds, relays, passes, *refs):
    count = 4 * adds + 2 * relays + passes
    ins, outs = list(refs[:count]), list(refs[count + waits :])
    if adds:
        part_x, part_y, given_a, given_b = ins[:4]
        to_x, to_y = outs[:2]
        cut = given_a.shape[2]
        low, high = pl.ds(0, cut), pl.ds(cut, cut)
        to_x[:, :, low] = part_x[:, :, low]
        to_x[:, :, high] = (
            part_x[:, :, high].astype(jnp.float32) + given_b[...].astype(jnp.float32)
        ).astype(jnp.bfloat16)
        to_y[:, :, low] = (
            part_y[:, :, low].astype(jnp.float32) + given_a[...].astype(jnp.float32)
        ).astype(jnp.bfloat16)
        to_y[:, :, high] = part_y[:, :, high]
        ins, outs = ins[4:], outs[2:]
    if relays:
        rows_x, rows_y = ins[:2]
        out_a, out_b = outs[:2]
        cut = out_a.shape[2]
        out_a[...] = rows_y[:, :, pl.ds(0, cut)]
        out_b[...] = rows_x[:, :, pl.ds(cut, out_b.shape[2])]
        ins, outs = ins[2:], outs[2:]
    if passes:
        outs[0][...] = ins[0][...]


def between(add, relay, block, after, ample):
    ins, outs = [], []
    if add is not None:
        ins += add
        outs += [add[0].shape, add[1].shape]
    if relay is not None:
        ins += relay
        count, rows, width = relay[0].shape
        cols = (width - 2 * EXPERTS) // 2
        outs += [(count, rows, cols + 2 * EXPERTS), (count, rows, cols)]
    if block is not None:
        ins += [block]
        outs += [block.shape]
    given = [int(a is not None) for a in (add, relay, block)]
    return pl.pallas_call(
        functools.partial(between_kernel, len(after), *given),
        grid=(1,),
        out_shape=[jax.ShapeDtypeStruct(o, jnp.bfloat16) for o in outs],
        in_specs=[at_once(i.shape) for i in ins]
        + [pl.BlockSpec(memory_space=pl.ANY)] * len(after),
        out_specs=[at_once(o) for o in outs],
        compiler_params=pltpu.CompilerParams(vmem_limit_bytes=VMEM_BYTES),
        cost_estimate=moves(ample),
    )(*ins, *after)


def add_up_kernel(count, waits, *refs):
    ins, outs = refs[:count], refs[count + waits :]
    for n, out in enumerate(outs):
        cut = pl.ds(n * out.shape[0], out.shape[0])
        total = ins[0][cut, :].astype(jnp.float32)
        for ref in ins[1:]:
            total = total + ref[cut, :].astype(jnp.float32)
        out[...] = total.astype(jnp.bfloat16)


def add_up(blocks, splits, *after):
    rows, width = blocks[0].shape
    out = jax.ShapeDtypeStruct((rows // splits, width), jnp.bfloat16)
    return pl.pallas_call(
        functools.partial(add_up_kernel, len(blocks), len(after)),
        grid=(1,),
        out_shape=[out] * splits,
        in_specs=[at_once((rows, width))] * len(blocks)
        + [pl.BlockSpec(memory_space=pl.ANY)] * len(after),
        out_specs=[at_once(out.shape)] * splits,
        compiler_params=pltpu.CompilerParams(vmem_limit_bytes=VMEM_BYTES),
        cost_estimate=moves(True),
    )(*blocks, *after)


def combine_kernel(count, waits, me, *refs):
    across_a, across_b = refs[3:5]
    slots, w_gate, w_up, w_down = refs[5:9]
    same, other, rows_in, hots, outs = refs[9 + waits :]
    step = pl.program_id(0)
    part, half = step // count, step % count
    rows, cols = rows_in.shape[0], across_b.shape[2]
    extra = pl.ds(cols, 2 * EXPERTS)
    hidden = w_gate.shape[2]
    features = w_gate.shape[1]
    at = pl.ds(pl.multiple_of(step * rows, 16), rows)
    for v in range(4):
        @pl.when(part == v)
        def _():
            left = refs[v] if v < 3 else across_a
            rows_in[:, pl.ds(0, cols)] = left[half, :, pl.ds(0, cols)]
            outs[at, pl.ds(2 * features, 2 * EXPERTS)] = left[half, :, extra]
            if v < 3:
                rows_in[:, pl.ds(cols, cols)] = left[half, :, pl.ds(cols + 2 * EXPERTS, cols)]
            else:
                rows_in[:, pl.ds(cols, cols)] = across_b[half]
    outs[at, pl.ds(0, features)] = dot_nn(rows_in[:, pl.ds(0, hidden)], w_down[0]).astype(jnp.bfloat16)
    outs[at, pl.ds(features, features)] = (
        dot_nt(rows_in[:, pl.ds(hidden, hidden)], w_gate[0])
        + dot_nt(rows_in[:, pl.ds(2 * hidden, hidden)], w_up[0])
    ).astype(jnp.bfloat16)
    hots[at, :] = jnp.where(one_hot(slots, rows), 1.0, 0.0).astype(jnp.bfloat16)

    @pl.when(step == pl.num_programs(0) - 1)
    def _():
        tokens, width = same.shape
        for ref, lo in ((same, 0), (other, tokens)):
            ref[...] = dot_tn(hots[:, pl.ds(lo, tokens)], outs[...]).astype(jnp.bfloat16)


def combine(me, given, slots, w_gate, w_up, w_down, after, halves, ample=True):
    count = len(halves)
    features, hidden = w_gate.shape[1:]
    rows = 2 * CAP
    tokens = slots.shape[2] // 2
    steps = 4 * count
    width = 2 * features + 2 * EXPERTS
    out = jax.ShapeDtypeStruct((tokens, width), jnp.bfloat16)
    return pl.pallas_call(
        functools.partial(combine_kernel, count, len(after)),
        grid_spec=pltpu.PrefetchScalarGridSpec(
            num_scalar_prefetch=1,
            grid=(steps,),
            in_specs=[whole(a.shape) for a in given]
            + [
                expert_block(slots.shape[1:], halves),
                expert_block((features, hidden), halves),
                expert_block((features, hidden), halves),
                expert_block((hidden, features), halves),
                *[pl.BlockSpec(memory_space=pl.ANY)] * len(after),
            ],
            out_specs=[whole(out.shape)] * 2,
            scratch_shapes=[
                pltpu.VMEM((rows, 3 * hidden), jnp.bfloat16),
                pltpu.VMEM((steps * rows, 2 * tokens), jnp.bfloat16),
                pltpu.VMEM((steps * rows, width), jnp.bfloat16),
            ],
        ),
        out_shape=(out, out),
        compiler_params=pltpu.CompilerParams(vmem_limit_bytes=VMEM_BYTES),
        cost_estimate=moves(ample),
    )(me, *given, slots, w_gate, w_up, w_down, *after)


def swap(value, axis, bits):
    count = lax.axis_size(axis)
    return lax.ppermute(value, axis, [(n, n ^ bits) for n in range(count)])


def grouped(tokens, gate_weight, up_weight, down_weight, routes, gate_levels, log_ratio, cotangent):
    block, features = tokens.shape
    per_device = gate_weight.shape[0]
    peers = lax.axis_size("expert")
    chips = peers // 2
    mine = lax.axis_index("expert")
    member = lax.axis_index("dp")
    me = member.astype(jnp.int32).reshape(1)

    ratio_weight = jnp.minimum(jnp.exp(log_ratio), clip_ratio)
    weighted = (ratio_weight[:, None] * cotangent.astype(jnp.float32)).astype(jnp.bfloat16)
    payload = jnp.concatenate([tokens, weighted], axis=1)
    arriving = swap(payload, "expert", 6)
    sames = {0: payload, 1: swap(payload, "expert", 2)}
    others = {0: swap(payload, "expert", 1)}

    local = mine * per_device + jnp.arange(per_device, dtype=jnp.int32)
    tri = (jnp.arange(block)[:, None] < jnp.arange(block)[None, :]).astype(jnp.bfloat16)

    def placed(picks):
        levels = picks[:, 1].astype(jnp.float32)
        fractions = levels / jnp.sum(levels, axis=1, keepdims=True)
        named = picks[:, 0][None] == local[:, None, None, None]
        share = jnp.sum(jnp.where(named, fractions[None], 0.0), axis=2)
        chosen = jnp.any(named, axis=2)
        place = jnp.einsum(
            "jst,tu->jsu", chosen.astype(jnp.bfloat16), tri, preferred_element_type=jnp.float32
        ).astype(jnp.int32)
        place = place + (jnp.arange(picks.shape[0], dtype=jnp.int32) % 2 * CAP)[None, :, None]
        slots = jnp.where(chosen, place, -1)
        pairs = (per_device, picks.shape[0] // 2, 1, 2 * block)
        return slots.reshape(pairs), share.reshape(pairs)

    picks = jnp.stack([routes.T, gate_levels.T])
    near = jnp.stack([picks, swap(picks, "expert", 1)])
    away = jnp.stack([swap(picks, "expert", 2 * o) for o in range(1, chips)])
    far = jnp.stack([away, swap(away, "expert", 1)], axis=1).reshape(-1, *picks.shape)
    near_slots, near_share = placed(near)
    far_slots, far_share = placed(far)

    weights = (gate_weight, up_weight, down_weight)
    chunks = [(0, (0,)), (3, (0, 1)), (2, (0, 1)), (1, (0, 1)), (0, (1,))]
    sums, adds, sent, got, relayed, blocks = {}, {}, {}, {}, {}, {}
    after = near_slots

    def slots_of(k):
        o = chunks[k][0]
        return far_slots[:, o - 1] if o else near_slots[:, 0]

    def share_of(k):
        o = chunks[k][0]
        return far_share[:, o - 1] if o else near_share[:, 0]

    def start_rows(k, *after):
        o, halves = chunks[k]
        own, part_x, part_y, across_a, across_b = partial_sums(
            me, sames[o], others[o], slots_of(k), *weights, after, halves, k > 0
        )
        sums[k] = own
        adds[k] = [part_x, part_y, swap(across_a, "dp", 1), swap(across_b, "dp", 2)]
        return own

    def move(k, r, *after, block=None):
        outs = between(adds.get(k), got.get(r), block, after, k != 0 and r != 0)
        if k in adds:
            sums[k] = sums[k], swap(outs[0], "dp", 1), swap(outs[1], "dp", 2)
        if r in got:
            at = 2 if k in adds else 0
            relayed[r] = swap(outs[at], "dp", 1), swap(outs[at + 1], "dp", 2)
        if block is not None:
            return outs[0], outs[-1], swap(outs[-1], "expert", 1)
        return outs[0]

    def turn_rows(k, *after):
        halves = chunks[k][1]
        first = 2 * member + halves[0]
        own_slot = lax.dynamic_slice_in_dim(slots_of(k), first, len(halves), 0)
        own_share = lax.dynamic_slice_in_dim(share_of(k), first, len(halves), 0)
        expert = (mine * per_device + first).astype(jnp.int32).reshape(1)
        sent[k] = middle(expert, *sums[k], own_slot, own_share, after, k > 0)
        got[k] = [swap(sent[k], "dp", 1), swap(sent[k], "dp", 2)]
        return sent[k]

    def finish_rows(k, *after):
        o, halves = chunks[k]
        given = (sent[k], *got[k], *relayed[k])
        same, other = combine(me, given, slots_of(k), *weights, after, halves)
        blocks[k] = [same, other]
        return same

    after = start_rows(0, after)
    after = move(0, None, after)
    after = turn_rows(0, after, far_slots, far_share)
    after, sames[3], others[3] = move(None, 0, after, block=arriving)
    sames[2] = swap(sames[3], "expert", 2)
    after = start_rows(1, after)
    after, sames[2], others[2] = move(1, None, after, block=sames[2])
    after = start_rows(2, after)
    after = turn_rows(1, after, *relayed[0])
    after = finish_rows(0, after)
    after, sames[1], others[1] = move(2, 1, after, block=sames[1])
    after = start_rows(3, after)
    after = turn_rows(2, after, *relayed[1])
    after = finish_rows(1, after)
    after, _, other = move(3, 2, after, block=blocks[1][1])
    after = start_rows(4, after)
    (after,) = add_up([blocks[1][0], other], 1, after, *relayed[2])
    hop = swap(after, "expert", 2)
    after = turn_rows(3, after, *adds[4][2:])
    after = finish_rows(2, after)
    after, _, other = move(4, 3, after, hop, block=blocks[2][1])
    after, second = add_up([blocks[2][0], other, hop], 2, after)
    far_low, far_high = swap(after, "expert", 4), swap(second, "expert", 4)
    after = finish_rows(3, second)
    after = turn_rows(4, after, far_low)
    after, _, other = move(None, None, after, block=blocks[3][1])
    (after,) = add_up([blocks[3][0], other], 1, after)
    near_back = swap(after, "expert", 2)
    after = move(None, 4, after)
    after = finish_rows(4, after)
    blocks[0][1] = swap(blocks[0][1], "expert", 1)
    _, _, blocks[4][1] = move(
        None, None, after, far_high, near_back, blocks[0][1], block=blocks[4][1]
    )
    far_back = jnp.concatenate([far_low, far_high], axis=0)
    total = sum(t.astype(jnp.float32) for t in (*blocks[0], *blocks[4], near_back, far_back))
    grads = total[:, 2 * features : 2 * features + EXPERTS] + total[:, 2 * features + EXPERTS :]
    hit = routes[:, :, None] == jnp.arange(EXPERTS, dtype=jnp.int32)
    gate_grad = jnp.sum(jnp.where(hit, grads[:, None, :], 0.0), axis=2)
    total = total[:, : 2 * features].astype(jnp.bfloat16)
    return total[:, :features], total[:, features:], gate_grad


def on_device(
    tokens, gate_weight, up_weight, down_weight, routes, gate_levels, log_ratio, cotangent
):
    local_tokens = tokens.shape[0]
    feature_slice = tokens.shape[1]
    hidden = gate_weight.shape[2]
    per_device = gate_weight.shape[0]
    peer_count = lax.axis_size("expert")
    slots_total = EXPERTS * CAP
    pick_ids = routes.reshape(-1)
    onehot_table = (pick_ids[:, None] == jnp.arange(EXPERTS, dtype=jnp.int32)[None, :]).astype(
        jnp.int32
    )
    earlier = jnp.cumsum(onehot_table, axis=0) - onehot_table
    position = jnp.sum(earlier * onehot_table, axis=1)
    target = pick_ids * CAP + position

    def pack_rows(values):
        packed = jnp.zeros((slots_total, feature_slice), jnp.bfloat16).at[target].set(values)
        return packed.reshape(peer_count, per_device * CAP, feature_slice)

    received = lax.all_to_all(
        pack_rows(jnp.repeat(tokens, TOPK, axis=0)),
        "expert",
        split_axis=0,
        concat_axis=0,
        tiled=True,
    )
    arrived = received.reshape(peer_count, per_device, CAP, feature_slice)
    gate_part = jnp.einsum(
        "sjcd,jdf->sjcf", arrived, gate_weight, preferred_element_type=jnp.float32
    ).reshape(-1, hidden)
    up_part = jnp.einsum(
        "sjcd,jdf->sjcf", arrived, up_weight, preferred_element_type=jnp.float32
    ).reshape(-1, hidden)
    gate_share, up_share = (
        lax.psum_scatter(gate_part, "dp", scatter_dimension=0, tiled=True),
        lax.psum_scatter(up_part, "dp", scatter_dimension=0, tiled=True),
    )
    activated = lax.all_gather(
        (jax.nn.silu(gate_share) * up_share).astype(jnp.bfloat16), "dp", axis=0, tiled=True
    )
    expert_out = jnp.einsum(
        "sjcf,jfd->sjcd",
        activated.reshape(peer_count, per_device, CAP, hidden),
        down_weight,
        preferred_element_type=jnp.float32,
    ).astype(jnp.bfloat16)
    returned = lax.all_to_all(
        expert_out.reshape(peer_count, per_device * CAP, feature_slice),
        "expert",
        split_axis=0,
        concat_axis=0,
        tiled=True,
    )
    picked = (
        returned.reshape(slots_total, feature_slice)[target]
        .reshape(local_tokens, TOPK, feature_slice)
        .astype(jnp.float32)
    )
    levels = gate_levels.astype(jnp.float32)
    fractions = levels / jnp.sum(levels, axis=1, keepdims=True)
    mixed_out = jnp.sum(fractions[:, :, None] * picked, axis=1).astype(jnp.bfloat16)
    ratio_weight = jnp.minimum(jnp.exp(log_ratio), clip_ratio)
    weighted = (ratio_weight[:, None] * cotangent.astype(jnp.float32)).astype(jnp.bfloat16)
    weighted_wide = weighted.astype(jnp.float32)[:, None, :]
    gate_grad = lax.psum(jnp.sum(weighted_wide * picked, axis=2), "dp")
    pick_grad = (
        (fractions[:, :, None] * weighted_wide).astype(jnp.bfloat16).reshape(-1, feature_slice)
    )
    back_rows = lax.all_to_all(
        pack_rows(pick_grad), "expert", split_axis=0, concat_axis=0, tiled=True
    )
    back_rows = back_rows.reshape(peer_count, per_device, CAP, feature_slice)
    hidden_part = jnp.einsum(
        "sjcd,jfd->sjcf", back_rows, down_weight, preferred_element_type=jnp.float32
    ).reshape(-1, hidden)
    hidden_grad = lax.psum_scatter(hidden_part, "dp", scatter_dimension=0, tiled=True)
    sigmoid_gate = jax.nn.sigmoid(gate_share)
    gate_back = (
        hidden_grad * up_share * sigmoid_gate * (1.0 + gate_share * (1.0 - sigmoid_gate))
    ).astype(jnp.bfloat16)
    up_back = (hidden_grad * gate_share * sigmoid_gate).astype(jnp.bfloat16)
    gate_rows, up_rows = (
        lax.all_gather(gate_back, "dp", axis=0, tiled=True),
        lax.all_gather(up_back, "dp", axis=0, tiled=True),
    )
    gate_rows = gate_rows.reshape(peer_count, per_device, CAP, hidden)
    up_rows = up_rows.reshape(peer_count, per_device, CAP, hidden)
    input_part = jnp.einsum(
        "sjcf,jdf->sjcd", gate_rows, gate_weight, preferred_element_type=jnp.float32
    )
    input_part = (
        input_part
        + jnp.einsum("sjcf,jdf->sjcd", up_rows, up_weight, preferred_element_type=jnp.float32)
    ).astype(jnp.bfloat16)
    input_back = lax.all_to_all(
        input_part.reshape(peer_count, per_device * CAP, feature_slice),
        "expert",
        split_axis=0,
        concat_axis=0,
        tiled=True,
    )
    back_picked = input_back.reshape(slots_total, feature_slice)[target].reshape(
        local_tokens, TOPK, feature_slice
    )
    token_grad = jnp.sum(back_picked.astype(jnp.float32), axis=1).astype(jnp.bfloat16)
    return (mixed_out, token_grad, gate_grad)


def solution(mesh):
    in_specs = (
        P("expert", "dp"),
        P("expert", "dp", None),
        P("expert", "dp", None),
        P("expert", None, "dp"),
        P("expert", None),
        P("expert", None),
        P("expert"),
        P("expert", "dp"),
    )
    out_specs = (P("expert", "dp"), P("expert", "dp"), P("expert", None))
    fits = mesh.shape["dp"] == 4 and mesh.shape["expert"] == 8
    return jax.shard_map(
        grouped if fits else on_device,
        mesh=mesh, in_specs=in_specs, out_specs=out_specs, check_vma=False,
    )
```
